32 devices in a mesh: gx: 4 (over y, core), gy: 8 (over z, x).
Axes of the slice: x: 2, y: 2, z: 4, core: 2. Of those that a mesh axis runs over, the one named last changes fastest.
Arguments:
- interface_conditions: float32 [8, 512, 1024], P(None, 'gx', 'gy'), may hold values from -3 to 1.5, as said below
- level_warmth_profile: float32 [512, 5, 10, 1024], P(('gx', 'gy')), may hold values from -2 to -0.1
- class_coverage_share: float32 [512, 5, 1024], P(('gx', 'gy')), may hold values from 0.02 to 0.4
- class_floe_depth: float32 [512, 5, 1024], P(('gx', 'gy')), may hold values from 0.5 to 4
- class_drift_depth: float32 [512, 5, 1024], P(('gx', 'gy')), may hold values from 0.05 to 0.5
- floe_drift_speed: float32 [2, 512, 1024], P(None, 'gx', 'gy'), may hold values from -3 to 3
- internal_tension_tensor: float32 [3, 512, 1024], P(None, 'gx', 'gy'), may hold values from -3 to 3
- external_drive: float32 [4, 512, 1024], P(None, 'gx', 'gy'), may hold values from -2 to 2
- floe_weight: float32 [512, 1024], P('gx', 'gy'), may hold values from 0.3 to 3
- floe_pressure: float32 [512, 1024], P('gx', 'gy'), may hold values from 0.2 to 2
- holder_lookup: int32 [512, 1], P(('gx', 'gy')), may hold values from 0 to 7, as said below
- ground_tile_marker: int32 [512], P(('gx', 'gy')), may hold values from 0 to 1, as said below
Outputs:
- revised_level_warmth: float32 [512, 5, 10, 1024], P(('gx', 'gy'))
- interface_exchanges: float32 [8, 512, 1024], P(None, 'gx', 'gy')
- velocity_new: float32 [2, 512, 1024], P(None, 'gx', 'gy')
- stress_new: float32 [3, 512, 1024], P(None, 'gx', 'gy')
The draws below stay inside these ranges and needn't reach their ends.
Inputs may be any that keep to these rules, and one draw needn't show every extreme that they name: `interface_conditions`: fields in order: ocean temperature in -0.2 to 0.1, salinity in 0.5 to 1, air temperature in -3 to -0.2, visible and near-infrared shortwave in 0 to 1, longwave in 0.5 to 1.5, snowfall and wind speed in 0 to 1. `holder_lookup`: each tile names one owner for at most 2 of its blocks. In every row of tiles there is one owner that every tile of the row names for exactly 2 blocks, none of them land. `ground_tile_marker`: 1 marks a land block.
All inputs are finite; a program needn't handle non-finite values.
Results may differ from the reference program's by a relative error of at most 0.0003.
Values sent between devices are 32-bit elements; how exact they have to be, the bound alone decides.
A program may use at most 128 MiB of HBM per device.

```python
import math
import jax
import jax.numpy as jnp
from jax import lax

BS = 32
BPX = 4
BPY = 4
CAP = 2
DEPTH_CLASSES = 5
FROZEN_LEVELS = 7
DRIFT_LEVELS = 3
POINT_QUANTITIES = 8
SUB = 4
TILE_POINTS = 1024
B = 16
HOLDER_PLACES = 16
NX = 512
NY = 1024
GRID_BLOCK_COUNT = 512
HOLDER_POSITIONS = 512
N_GX = 4
N_GY = 8


def draw_interface_conditions(key, part):
    lower_ends = jnp.array([-0.2, 0.5, -3.0, 0.0, 0.0, 0.5, 0.0, 0.0], jnp.float32)
    upper_ends = jnp.array([0.1, 1.0, -0.2, 1.0, 1.0, 1.5, 1.0, 1.0], jnp.float32)
    unit_draw = jax.random.uniform(key, (POINT_QUANTITIES, NX, NY), jnp.float32)
    return lower_ends[:, None, None] + (upper_ends - lower_ends)[:, None, None] * unit_draw


def route_plan(key):
    base_key = jax.random.fold_in(key, 11)
    pick_key, place_key, land_key = jax.random.split(base_key, 3)
    device_count = N_GX * N_GY
    favoured = jax.random.randint(pick_key, (N_GX,), 0, N_GY)
    favoured_dev = jnp.repeat(favoured, N_GY)
    entry_owner = jnp.arange(N_GY * CAP, dtype=jnp.int32) // CAP

    def one_device(device_key, chosen):
        first_key, second_key = jax.random.split(device_key)
        shuffled = jax.random.permutation(first_key, entry_owner)
        pushed = (shuffled == chosen).astype(jnp.int32)
        arranged = shuffled[jnp.argsort(pushed, stable=True)]
        listed = jnp.concatenate([jnp.full((CAP,), chosen, jnp.int32), arranged[:B - CAP]])
        return jax.random.permutation(second_key, listed)
    owners = jax.vmap(one_device)(jax.random.split(place_key, device_count), favoured_dev)
    land_flag = (jax.random.randint(land_key, (device_count, B), 0, 4) == 0) & (owners != favoured_dev[:, None])
    return (owners.reshape(GRID_BLOCK_COUNT, 1).astype(jnp.int32), land_flag.astype(jnp.int32).reshape(GRID_BLOCK_COUNT))


def draw_holder_lookup(key, part):
    return route_plan(key)[0]


def draw_ground_tile_marker(key, part):
    return route_plan(key)[1]


def steps_of(stream_key, extent, cuts, low, top_value):
    loudness = 1.0
    for axis_at, parts in cuts:
        steps = jax.random.uniform(jax.random.fold_in(jax.random.fold_in(stream_key, 6), axis_at), (parts,), jnp.float32, low / len(cuts), top_value / len(cuts))
        loudness = loudness * jnp.repeat(jnp.exp(steps), extent[axis_at] // parts).reshape((-1,) + (1,) * (len(extent) - 1 - axis_at))
    return loudness


def centred(key, shape, scale, limit, pieces=(), kind=jnp.bfloat16):
    result = scale * jax.random.normal(key, shape, jnp.float32)
    if pieces:
        result = result * steps_of(key, shape, pieces, -0.22, 0.18)
    return jnp.clip(result, -limit, limit).astype(kind)


def setup_inputs(seed: int = 0) -> dict:
    seeds = jax.random.split(jax.random.key(seed), 13)
    return {
        "interface_conditions": draw_interface_conditions(jax.random.fold_in(seeds[12], 71), 0),
        "level_warmth_profile": jnp.clip(-2.0 + 1.9 * jax.random.uniform(seeds[1], (HOLDER_POSITIONS, DEPTH_CLASSES, DRIFT_LEVELS + FROZEN_LEVELS, TILE_POINTS), jnp.float32) ** steps_of(seeds[1], (HOLDER_POSITIONS, DEPTH_CLASSES, DRIFT_LEVELS + FROZEN_LEVELS, TILE_POINTS), ((0, 32),), -0.2, 0.2), -2.0, -0.1),
        "class_coverage_share": jnp.clip(0.02 + 0.38 * jax.random.uniform(seeds[2], (HOLDER_POSITIONS, DEPTH_CLASSES, TILE_POINTS), jnp.float32) ** steps_of(seeds[2], (HOLDER_POSITIONS, DEPTH_CLASSES, TILE_POINTS), ((0, 32),), -0.2, 0.2), 0.02, 0.4),
        "class_floe_depth": jnp.clip(jnp.exp(math.log(4.0) - 2.0794415 * jax.random.uniform(seeds[3], (HOLDER_POSITIONS, DEPTH_CLASSES, TILE_POINTS), jnp.float32) ** steps_of(seeds[3], (HOLDER_POSITIONS, DEPTH_CLASSES, TILE_POINTS), ((0, 32),), -0.2, 0.2)), 0.5, 4.0),
        "class_drift_depth": jnp.clip(jnp.exp(math.log(0.5) - 2.3025851 * jax.random.uniform(seeds[4], (HOLDER_POSITIONS, DEPTH_CLASSES, TILE_POINTS), jnp.float32) ** steps_of(seeds[4], (HOLDER_POSITIONS, DEPTH_CLASSES, TILE_POINTS), ((0, 32),), -0.2, 0.2)), 0.05, 0.5),
        "floe_drift_speed": centred(seeds[5], (2, NX, NY), 0.5, 3.0, ((1, 4), (2, 8)), jnp.float32),
        "internal_tension_tensor": centred(seeds[6], (3, NX, NY), 0.5, 3.0, ((1, 4), (2, 8)), jnp.float32),
        "external_drive": centred(seeds[7], (4, NX, NY), 0.3, 2.0, ((1, 4), (2, 8)), jnp.float32),
        "floe_weight": jnp.clip(jnp.exp(math.log(3.0) - 2.3025851 * jax.random.uniform(seeds[8], (NX, NY), jnp.float32) ** steps_of(seeds[8], (NX, NY), ((0, 4), (1, 8)), -0.2, 0.2)), 0.3, 3.0),
        "floe_pressure": jnp.clip(jnp.exp(math.log(2.0) - 2.3025851 * jax.random.uniform(seeds[9], (NX, NY), jnp.float32) ** steps_of(seeds[9], (NX, NY), ((0, 4), (1, 8)), -0.2, 0.2)), 0.2, 2.0),
        "holder_lookup": draw_holder_lookup(jax.random.fold_in(seeds[12], 71), 0),
        "ground_tile_marker": draw_ground_tile_marker(jax.random.fold_in(seeds[12], 71), 0),
    }


RELAX_RATE = 0.5
ECC_SQUARED = 4.0
DELTA_FLOOR = 0.04
MOTION_STEP = 0.5
WATER_DRAG = 1.0
CORIOLIS = 0.3
HEAT_STEP = 0.5
SNOW_COND = 0.3
SNOW_GAIN = 0.3
GROWTH_RATE = 0.05

def column_step(layer_temp, cat_area, cat_thick, cat_snow, forcing_fields):
    ocean_temp = forcing_fields[:, 0:1]
    salinity = forcing_fields[:, 1:2]
    air_temp = forcing_fields[:, 2:3]
    visible = forcing_fields[:, 3:4]
    near_red = forcing_fields[:, 4:5]
    longwave = forcing_fields[:, 5:6]
    snowfall = forcing_fields[:, 6:7]
    wind_speed = forcing_fields[:, 7:8]
    snow_depth = cat_snow + SNOW_GAIN * snowfall
    layer_total = DRIFT_LEVELS + FROZEN_LEVELS
    depths = []
    heat_caps = []
    resist = []
    for layer_num in range(layer_total):
        old_temp = layer_temp[:, :, layer_num]
        if layer_num < DRIFT_LEVELS:
            layer_depth = snow_depth / DRIFT_LEVELS
            heat_cap = jnp.ones_like(layer_depth)
            conduct = SNOW_COND
        else:
            brine_term = salinity * (0.2 + 0.1 * (layer_num - DRIFT_LEVELS))
            layer_depth = cat_thick / FROZEN_LEVELS
            heat_cap = 1.0 + 0.2 * brine_term / (old_temp * old_temp + 0.1)
            conduct = 2.0 + 0.1 * brine_term / (old_temp - 0.5)
        depths.append(layer_depth)
        heat_caps.append(heat_cap)
        resist.append(layer_depth / conduct)
    top_cond = 1.0 / (0.5 * resist[0] + 1.0 / (1.0 + 2.0 * wind_speed))
    bottom_cond = 2.0 / resist[-1]
    inner_cond = [1.0 / (0.5 * (resist[layer_num] + resist[layer_num + 1])) for layer_num in range(layer_total - 1)]
    cond_above = [top_cond] + inner_cond
    cond_below = inner_cond + [bottom_cond]
    sweep_ratio = []
    sweep_value = []
    for layer_num in range(layer_total):
        mass_term = heat_caps[layer_num] * depths[layer_num] / HEAT_STEP
        diagonal = mass_term + cond_above[layer_num] + cond_below[layer_num]
        source = mass_term * layer_temp[:, :, layer_num]
        if layer_num == 0:
            source = source + top_cond * air_temp + 0.25 * visible + 0.45 * near_red + 0.3 * longwave
        if layer_num == layer_total - 1:
            source = source + bottom_cond * ocean_temp
        if layer_num > 0:
            pivot_term = diagonal - cond_above[layer_num] * sweep_ratio[-1]
            carried = source + cond_above[layer_num] * sweep_value[-1]
        else:
            pivot_term = diagonal
            carried = source
        sweep_ratio.append(cond_below[layer_num] / pivot_term)
        sweep_value.append(carried / pivot_term)
    solved = [sweep_value[-1]]
    for layer_num in range(layer_total - 2, -1, -1):
        solved.insert(0, sweep_value[layer_num] + sweep_ratio[layer_num] * solved[0])
    advanced_warmth = jnp.stack(solved, axis=2)
    bottom_flux = bottom_cond * (solved[-1] - ocean_temp)
    growth = -GROWTH_RATE * bottom_flux
    energy = heat_caps[0] * depths[0] * solved[0]
    for layer_num in range(1, layer_total):
        energy = energy + heat_caps[layer_num] * depths[layer_num] * solved[layer_num]
    light_through = 0.7 * visible * jnp.exp(-5.0 * snow_depth - 1.5 * cat_thick)
    flux_terms = [bottom_flux, top_cond * (air_temp - solved[0]), light_through, solved[0], snow_depth, cat_thick + growth, 0.1 * energy, growth * salinity]
    slot_fluxes = jnp.stack([lax.optimization_barrier(jnp.sum(cat_area * term_value, axis=1)) for term_value in flux_terms], axis=1)
    return (advanced_warmth, slot_fluxes)

def strain_rates(drift_kinematics):
    east_vel = drift_kinematics[0]
    north_vel = drift_kinematics[1]
    du_x = 0.5 * (east_vel[2:, 1:-1] - east_vel[:-2, 1:-1])
    du_y = 0.5 * (east_vel[1:-1, 2:] - east_vel[1:-1, :-2])
    dv_x = 0.5 * (north_vel[2:, 1:-1] - north_vel[:-2, 1:-1])
    dv_y = 0.5 * (north_vel[1:-1, 2:] - north_vel[1:-1, :-2])
    return (du_x + dv_y, du_x - dv_y, du_y + dv_x)

def update_stress(stress_old, strength, drift_kinematics):
    diverge, tension, shearing = strain_rates(drift_kinematics)
    spread = jnp.sqrt(diverge * diverge + (tension * tension + shearing * shearing) / ECC_SQUARED + DELTA_FLOOR)
    ratio = strength / spread
    first = (stress_old[0] + RELAX_RATE * ratio * (diverge - spread)) / (1.0 + RELAX_RATE)
    second = (stress_old[1] + RELAX_RATE * ratio * tension / ECC_SQUARED) / (1.0 + RELAX_RATE)
    third = (stress_old[2] + RELAX_RATE * ratio * shearing / (2.0 * ECC_SQUARED)) / (1.0 + RELAX_RATE)
    return jnp.stack([first, second, third])

def stress_force(stress_pad):
    stress_sum = stress_pad[0] + stress_pad[1]
    differ = stress_pad[0] - stress_pad[1]
    shear_part = stress_pad[2]
    force_x = 0.25 * (stress_sum[2:, 1:-1] - stress_sum[:-2, 1:-1]) + 0.5 * (shear_part[1:-1, 2:] - shear_part[1:-1, :-2])
    force_y = 0.25 * (differ[1:-1, 2:] - differ[1:-1, :-2]) + 0.5 * (shear_part[2:, 1:-1] - shear_part[:-2, 1:-1])
    return (force_x, force_y)

def update_motion(drift_kinematics, force_x, force_y, floe_weight, external_drive, water_mask):
    east_vel = drift_kinematics[0]
    north_vel = drift_kinematics[1]
    denominator = floe_weight + MOTION_STEP * WATER_DRAG
    new_east = (floe_weight * east_vel + MOTION_STEP * (force_x + external_drive[0] + WATER_DRAG * external_drive[2] + CORIOLIS * floe_weight * north_vel)) / denominator
    new_north = (floe_weight * north_vel + MOTION_STEP * (force_y + external_drive[1] + WATER_DRAG * external_drive[3] - CORIOLIS * floe_weight * east_vel)) / denominator
    return jnp.stack([new_east * water_mask, new_north * water_mask])

def reference(interface_conditions, level_warmth_profile, class_coverage_share, class_floe_depth, class_drift_depth, floe_drift_speed, internal_tension_tensor, external_drive, floe_weight, floe_pressure, holder_lookup, ground_tile_marker):
    patch_total = N_GX * N_GY
    tiles_row = HOLDER_PLACES // CAP
    blocks_of_grid = interface_conditions.reshape(POINT_QUANTITIES, N_GX, BPX, BS, N_GY, BPY, BS).transpose(1, 4, 2, 5, 0, 3, 6).reshape(GRID_BLOCK_COUNT, POINT_QUANTITIES, TILE_POINTS)
    target = holder_lookup[:, 0].reshape(patch_total, B)
    slot_covered = (1 - ground_tile_marker).reshape(patch_total, B)
    later = lax.broadcasted_iota(jnp.int32, (B, B), 1) < lax.broadcasted_iota(jnp.int32, (B, B), 0)
    matching = (target[:, :, None] == target[:, None, :]) & (slot_covered[:, None, :] == 1) & later[None]
    order_rank = lax.optimization_barrier(jnp.sum(matching.astype(jnp.int32), axis=2))
    tile_num = lax.broadcasted_iota(jnp.int32, (patch_total, B), 0)
    block_slot = (tile_num // tiles_row * tiles_row + target) * HOLDER_PLACES + tile_num % tiles_row * CAP + order_rank
    block_slot = jnp.where(slot_covered == 1, block_slot, HOLDER_POSITIONS).reshape(GRID_BLOCK_COUNT).astype(jnp.int32)
    quantities_each_position = jnp.zeros((HOLDER_POSITIONS, POINT_QUANTITIES, TILE_POINTS), jnp.float32).at[block_slot].set(blocks_of_grid, mode='drop')
    position_occupied = jnp.zeros((HOLDER_POSITIONS,), jnp.float32).at[block_slot].set(1.0, mode='drop')

    def by_holder(bundle):
        layer_temp, cat_area, cat_thick, cat_snow, owner_fields, owner_filled = bundle
        advanced_warmth, slot_fluxes = column_step(layer_temp, cat_area, cat_thick, cat_snow, owner_fields)
        kept = jnp.where(owner_filled[:, None, None, None] > 0.5, advanced_warmth, layer_temp)
        return (kept, slot_fluxes)
    renewed_heat_levels, outgoing_exchange_quantities = lax.map(by_holder, (level_warmth_profile.reshape(patch_total, HOLDER_PLACES, DEPTH_CLASSES, DRIFT_LEVELS + FROZEN_LEVELS, TILE_POINTS), class_coverage_share.reshape(patch_total, HOLDER_PLACES, DEPTH_CLASSES, TILE_POINTS), class_floe_depth.reshape(patch_total, HOLDER_PLACES, DEPTH_CLASSES, TILE_POINTS), class_drift_depth.reshape(patch_total, HOLDER_PLACES, DEPTH_CLASSES, TILE_POINTS), quantities_each_position.reshape(patch_total, HOLDER_PLACES, POINT_QUANTITIES, TILE_POINTS), position_occupied.reshape(patch_total, HOLDER_PLACES)))
    revised_level_warmth = renewed_heat_levels.reshape(HOLDER_POSITIONS, DEPTH_CLASSES, DRIFT_LEVELS + FROZEN_LEVELS, TILE_POINTS)
    flattened_fluxes = jnp.concatenate([outgoing_exchange_quantities.reshape(HOLDER_POSITIONS, 8, TILE_POINTS), jnp.zeros((1, 8, TILE_POINTS), jnp.float32)], axis=0)
    block_fluxes = jnp.take(flattened_fluxes, block_slot, axis=0)
    interface_exchanges = block_fluxes.reshape(N_GX, N_GY, BPX, BPY, 8, BS, BS).transpose(4, 0, 2, 5, 1, 3, 6).reshape(8, NX, NY)
    land_grid = ground_tile_marker.reshape(N_GX, N_GY, BPX, BPY).transpose(0, 2, 1, 3).reshape(N_GX * BPX, N_GY * BPY)
    water_mask = jnp.repeat(jnp.repeat(1.0 - land_grid.astype(jnp.float32), BS, axis=0), BS, axis=1)
    drift_kinematics = floe_drift_speed
    tension_components = internal_tension_tensor
    for subcycle in range(SUB):
        padded = jnp.pad(drift_kinematics, ((0, 0), (1, 1), (1, 1)))
        tension_components = update_stress(tension_components, floe_pressure, padded)
        force_x, force_y = stress_force(jnp.pad(tension_components, ((0, 0), (1, 1), (1, 1))))
        drift_kinematics = update_motion(drift_kinematics, force_x, force_y, floe_weight, external_drive, water_mask)
    return (revised_level_warmth, interface_exchanges, drift_kinematics, tension_components)
```

```python
import functools

import jax
import jax.numpy as jnp
from jax import lax
from jax.experimental import pallas as pl
from jax.experimental.pallas import tpu as pltpu
from jax.sharding import PartitionSpec as P

MESH = pl.DeviceIdType.MESH
BS = 32
BPX = 4
BPY = 4
CAP = 2
ICE = 7
SNOW = 3
LAYERS = 10
CLASSES = 5
SUB = 4
B = 16
TILE = 128
SENT = 6
BACK = 7
EVP = 10
HALO = 8
ROWS = TILE + 4 * HALO
VMEM_LIMIT = 48 * 1024 * 1024


def rcp(x):
    r = pl.reciprocal(x, approx=True)
    return r * (2.0 - x * r)


def swap_groups(x):
    group = lax.broadcasted_iota(jnp.int32, x[0].shape, 1) // BS
    even = (group % 2) == 0
    low = group < 2
    y = [None] * 4
    for a in (0, 2):
        y[a] = jnp.where(even, x[a], pltpu.roll(x[a + 1], BS, 1))
        y[a + 1] = jnp.where(even, pltpu.roll(x[a], TILE - BS, 1), x[a + 1])
    z = [None] * 4
    for a in (0, 1):
        z[a] = jnp.where(low, y[a], pltpu.roll(y[a + 2], 2 * BS, 1))
        z[a + 2] = jnp.where(low, pltpu.roll(y[a], 2 * BS, 1), y[a + 2])
    return z


def evp_steps(ext):
    bands = [2 * HALO * i + HALO for i in range((TILE + 2 * HALO) // (2 * HALO))]
    size = 2 * HALO
    third = 1.0 / 1.5

    def d_row(f, r):
        return 0.5 * (ext[f, r + 1 : r + 1 + size, :] - ext[f, r - 1 : r - 1 + size, :])

    def d_lane(x):
        width = x.shape[1]
        return 0.5 * (pltpu.roll(x, width - 1, 1) - pltpu.roll(x, 1, 1))

    def step(_, carry):
        for r in bands:
            here = slice(r, r + size)
            ux, uy = d_row(0, r), d_lane(ext[0, here, :])
            vx, vy = d_row(1, r), d_lane(ext[1, here, :])
            diverge, tension, shearing = ux + vy, ux - vy, uy + vx
            square = diverge * diverge + 0.25 * (tension * tension + shearing * shearing) + 0.04
            inverse = lax.rsqrt(square)
            push = ext[9, here, :]
            scaled = push * inverse
            ext[2, here, :] = third * ext[2, here, :] + (scaled * diverge - push)
            ext[3, here, :] = third * ext[3, here, :] + 0.25 * (scaled * tension)
            ext[4, here, :] = third * ext[4, here, :] + 0.125 * (scaled * shearing)
        for r in bands:
            here = slice(r, r + size)
            force_x = 0.5 * (d_row(2, r) + d_row(3, r)) + d_lane(ext[4, here, :])
            force_y = 0.5 * d_lane(ext[2, here, :] - ext[3, here, :]) + d_row(4, r)
            east, north = ext[0, here, :], ext[1, here, :]
            half, keep = ext[5, here, :], ext[6, here, :]
            ext[0, here, :] = keep * (east + 0.15 * north) + half * force_x + ext[7, here, :]
            ext[1, here, :] = keep * (north - 0.15 * east) + half * force_y + ext[8, here, :]
        return carry

    lax.fori_loop(0, SUB, step, 0)


def forward_kernel(
    n, m,
    cond, vel, stress, drive, weight, pressure, holder, marker,
    slots, vel_out, stress_out,
    blk, send, ext, pack_w, pack_e, top, bottom, got_w, got_e, got_t, got_b,
    send_sem, recv_sem, hsend_sem, hrecv_sem,
):
    gx, gy = lax.axis_index("gx"), lax.axis_index("gy")
    up, down = lax.rem(gx + m - 1, m), lax.rem(gx + 1, m)
    left, right = lax.rem(gy + n - 1, n), lax.rem(gy + 1, n)
    around = [(up, gy), (down, gy), (up, left), (up, right), (down, left), (down, right)]

    barrier = pltpu.get_barrier_semaphore()

    def greet(k, carry):
        pl.semaphore_signal(
            barrier, inc=1, device_id=(gx, lax.rem(gy + k, n)), device_id_type=MESH
        )
        return carry

    lax.fori_loop(1, n, greet, 0)
    for device in around:
        pl.semaphore_signal(barrier, inc=1, device_id=device, device_id_type=MESH)

    for bx in range(BPX):
        def part(f, q):
            return cond[f, pl.ds(BS * bx + q, 8, stride=4), :]

        for at, f in enumerate((0, 1, 2, None, 6, 7)):
            if f is None:
                pieces = [
                    0.25 * part(3, q) + 0.45 * part(4, q) + 0.3 * part(5, q) for q in range(4)
                ]
            else:
                pieces = [part(f, q) for q in range(4)]
            for by, piece in enumerate(swap_groups(pieces)):
                blk[bx * BPY + by, at] = piece

    def fill(o, carry):
        count = jnp.int32(0)
        first = jnp.int32(0)
        second = jnp.int32(0)
        for b in range(B):
            hit = jnp.where(holder[b, 0] == o, 1 - marker[b], 0)
            first = first + jnp.where(count == 0, hit * b, 0)
            second = second + jnp.where(count == 1, hit * b, 0)
            count = count + hit
        has_first = jnp.where(count > 0, 1.0, 0.0)
        has_second = jnp.where(count > 1, 1.0, 0.0)
        send[o, 0] = blk[first] * has_first
        send[o, 1] = blk[second] * has_second
        return carry

    lax.fori_loop(0, n, fill, 0)
    slots[gy] = send[gy]

    pl.semaphore_wait(barrier, n - 1 + len(around))

    def parcel(k):
        o = lax.rem(gy + k, n)
        return pltpu.make_async_remote_copy(
            src_ref=send.at[o], dst_ref=slots.at[gy],
            send_sem=send_sem.at[k], recv_sem=recv_sem.at[k],
            device_id=(gx, o), device_id_type=MESH,
        )

    def launch(k, carry):
        parcel(k).start()
        return carry

    lax.fori_loop(1, n, launch, 0)

    inner = slice(2 * HALO, 2 * HALO + TILE)
    ext[...] = jnp.zeros_like(ext)
    for f in range(2):
        ext[f, inner, :TILE] = vel[f]
    for f in range(3):
        ext[2 + f, inner, :TILE] = stress[f]
    column = lax.broadcasted_iota(jnp.int32, (BS, TILE), 1) // BS
    for bx in range(BPX):
        rows = slice(BS * bx, BS * bx + BS)
        into = slice(2 * HALO + BS * bx, 2 * HALO + BS * bx + BS)
        water = jnp.zeros((BS, TILE), jnp.float32)
        for by in range(BPY):
            sea = (1 - marker[bx * BPY + by]).astype(jnp.float32)
            water = jnp.where(column == by, sea, water)
        w = weight[rows, :]
        share = water * rcp(w + 0.5)
        half = 0.5 * share
        ext[5, into, :TILE] = half
        ext[6, into, :TILE] = share * w
        ext[7, into, :TILE] = half * (drive[0, rows, :] + drive[2, rows, :])
        ext[8, into, :TILE] = half * (drive[1, rows, :] + drive[3, rows, :])
        ext[9, into, :TILE] = pressure[rows, :] * (1.0 / 3.0)

    lane = lax.broadcasted_iota(jnp.int32, (TILE, TILE), 1)
    packed_w = jnp.zeros((TILE, TILE), jnp.float32)
    packed_e = jnp.zeros((TILE, TILE), jnp.float32)
    for f in range(EVP):
        own = (lane // HALO) == f
        x = ext[f, inner, :TILE]
        packed_w = jnp.where(own, pltpu.roll(x, HALO * f, 1) if f else x, packed_w)
        packed_e = jnp.where(own, pltpu.roll(x, HALO * (f + 1), 1), packed_e)
        top[f] = ext[f, 2 * HALO : 3 * HALO, :TILE]
        bottom[f] = ext[f, HALO + TILE : 2 * HALO + TILE, :TILE]
    pack_w[...] = packed_w
    pack_e[...] = packed_e

    head, tail = pl.ds(0, HALO), pl.ds(TILE - HALO, HALO)
    first, middle, last = pl.ds(0, HALO), pl.ds(HALO, TILE), pl.ds(HALO + TILE, HALO)
    halos = [
        (pack_w, got_e.at[middle], (gx, left)),
        (pack_e, got_w.at[middle], (gx, right)),
        (top, got_b, (up, gy)),
        (bottom, got_t, (down, gy)),
        (pack_w.at[head], got_e.at[last], (up, left)),
        (pack_e.at[head], got_w.at[last], (up, right)),
        (pack_w.at[tail], got_e.at[first], (down, left)),
        (pack_e.at[tail], got_w.at[first], (down, right)),
    ]
    copies = [
        pltpu.make_async_remote_copy(
            src_ref=src, dst_ref=dst, send_sem=hsend_sem.at[i], recv_sem=hrecv_sem.at[i],
            device_id=device, device_id_type=MESH,
        )
        for i, (src, dst, device) in enumerate(halos)
    ]
    for copy in copies:
        copy.start()
    for copy in copies:
        copy.wait()

    on_top = jnp.where(gx > 0, 1.0, 0.0)
    on_bottom = jnp.where(gx < m - 1, 1.0, 0.0)
    on_left = jnp.where(gy > 0, 1.0, 0.0)
    on_right = jnp.where(gy < n - 1, 1.0, 0.0)
    tall = TILE + 2 * HALO
    row = lax.broadcasted_iota(jnp.int32, (tall, TILE), 0)
    lane = lax.broadcasted_iota(jnp.int32, (tall, TILE), 1)
    upright = jnp.where(row < HALO, on_top, jnp.where(row < HALO + TILE, 1.0, on_bottom))
    sided_e = got_e[...] * (upright * on_right)
    sided_w = got_w[...] * (upright * on_left)
    for f in range(EVP):
        ext[f, HALO : 2 * HALO, :TILE] = got_t[f] * on_top
        ext[f, 2 * HALO + TILE : 3 * HALO + TILE, :TILE] = got_b[f] * on_bottom
        from_e = pltpu.roll(sided_e, TILE - HALO * f, 1) if f else sided_e
        from_w = pltpu.roll(sided_w, TILE - HALO * (f + 1), 1)
        ext[f, HALO : HALO + tall, TILE:] = jnp.where(
            lane < HALO, from_e, jnp.where(lane >= TILE - HALO, from_w, 0.0)
        )

    evp_steps(ext)
    for f in range(2):
        vel_out[f] = ext[f, inner, :TILE]
    for f in range(3):
        stress_out[f] = ext[2 + f, inner, :TILE]

    def finish(k, carry):
        parcel(k).wait()
        return carry

    lax.fori_loop(1, n, finish, 0)


def column_kernel(
    n, slots, warmth, share, thick, drift, warmth_out, fluxes,
    held, classes, in_sem, out_sem, class_sem,
):
    held5 = held.reshape(n * CAP, CLASSES, 8, 16, TILE)
    classes5 = classes.reshape(3, n * CAP, 8, 8, TILE)

    def class_copies():
        return [
            pltpu.make_async_copy(
                array.at[:, :, pl.ds(TILE * j, TILE)],
                classes5.at[i, :, j, pl.ds(0, CLASSES), :],
                class_sem.at[i, j],
            )
            for i, array in enumerate((share, thick, drift))
            for j in range(8)
        ]

    def moves(t, array, sem, out):
        group = pl.ds(CAP * t, CAP)
        copies = []
        for j in range(8):
            far = array.at[group, :, :, pl.ds(TILE * j, TILE)]
            near = held5.at[group, :, j, pl.ds(0, LAYERS), :]
            src, dst = (near, far) if out else (far, near)
            copies.append(pltpu.make_async_copy(src, dst, sem.at[t, j]))
        return copies

    for copy in class_copies():
        copy.start()

    def fetch(t, carry):
        for copy in moves(t, warmth, in_sem, False):
            copy.start()
        return carry

    lax.fori_loop(0, n, fetch, 0)
    for copy in class_copies():
        copy.wait()

    def one_slot(t, r):
        s = t * CAP + r
        ocean, salt, air, source, snowfall, wind = [slots[t, r, f] for f in range(SENT)]
        filled = salt > 0.25
        air_resist = rcp(1.0 + 2.0 * wind)
        sums = None
        for c in range(CLASSES):
            area, floe, lying = [
                classes[pl.ds(i * (n * CAP * 64) + s * 64 + c, 8, stride=8), :] for i in range(3)
            ]
            base = (s * CLASSES + c) * 128

            def place(l):
                return pl.ds(base + l, 8, stride=16)

            snow = lying + 0.3 * snowfall
            depth = floe * (1.0 / ICE)
            twice = 2.0 * depth
            snow_mass = snow * (2.0 / 3.0)
            snow_resist = snow * (1.0 / 0.9)
            snow_cond = rcp(snow_resist)
            top = rcp(0.5 * snow_resist + air_resist)
            above, resist = top, snow_resist
            ratios, values = [], []
            content = None
            for l in range(LAYERS):
                old = held[place(l), :]
                if l < SNOW:
                    mass = snow_mass
                else:
                    brine = salt * (0.2 + 0.1 * (l - SNOW))
                    mass = twice + twice * (0.2 * brine) * rcp(old * old + 0.1)
                if l < SNOW - 1:
                    below = snow_cond
                elif l < LAYERS - 1:
                    brine = salt * (0.2 + 0.1 * (l + 1 - SNOW))
                    shifted = held[place(l + 1), :] - 0.5
                    later = depth * shifted * rcp(2.0 * shifted + 0.1 * brine)
                    below = 2.0 * rcp(resist + later)
                    resist = later
                else:
                    below = 2.0 * rcp(resist)
                held_heat = mass * old
                content = held_heat if content is None else content + held_heat
                carried = held_heat
                pivot = mass + above + below
                if l == 0:
                    carried = carried + top * air + source
                if l == LAYERS - 1:
                    carried = carried + below * ocean
                if l > 0:
                    pivot = pivot - above * ratios[-1]
                    carried = carried + above * values[-1]
                inverse = rcp(pivot)
                ratios.append(below * inverse)
                values.append(carried * inverse)
                above = below
            new = values[-1]
            last = new
            held[place(LAYERS - 1), :] = jnp.where(filled, new, held[place(LAYERS - 1), :])
            for l in range(LAYERS - 2, -1, -1):
                new = values[l] + ratios[l] * new
                held[place(l), :] = jnp.where(filled, new, held[place(l), :])
            bottom_flux = below * (last - ocean)
            top_flux = top * (air - new)
            terms = [
                bottom_flux, top_flux, jnp.exp(-5.0 * lying - 1.5 * floe), new, snow, floe,
                0.05 * (content + top_flux - bottom_flux + source),
            ]
            terms = [area * term for term in terms]
            sums = terms if sums is None else [a + b for a, b in zip(sums, terms)]
        for f in range(BACK):
            fluxes[t, r, f] = sums[f]

    def tile(t, carry):
        for copy in moves(t, warmth, in_sem, False):
            copy.wait()
        for r in range(CAP):
            one_slot(t, r)
        for copy in moves(t, warmth_out, out_sem, True):
            copy.start()
        return carry

    lax.fori_loop(0, n, tile, 0)

    def flush(t, carry):
        for copy in moves(t, warmth_out, out_sem, True):
            copy.wait()
        return carry

    lax.fori_loop(0, n, flush, 0)


def return_kernel(n, fluxes, cond, holder, marker, out, got, send_sem, recv_sem):
    gx, gy = lax.axis_index("gx"), lax.axis_index("gy")
    barrier = pltpu.get_barrier_semaphore()

    def greet(k, carry):
        pl.semaphore_signal(
            barrier, inc=1, device_id=(gx, lax.rem(gy + k, n)), device_id_type=MESH
        )
        return carry

    lax.fori_loop(1, n, greet, 0)
    got[gy] = fluxes[gy]
    pl.semaphore_wait(barrier, n - 1)

    def parcel(k):
        o = lax.rem(gy + k, n)
        return pltpu.make_async_remote_copy(
            src_ref=fluxes.at[o], dst_ref=got.at[gy],
            send_sem=send_sem.at[k], recv_sem=recv_sem.at[k],
            device_id=(gx, o), device_id_type=MESH,
        )

    def launch(k, carry):
        parcel(k).start()
        return carry

    def finish(k, carry):
        parcel(k).wait()
        return carry

    lax.fori_loop(1, n, launch, 0)
    lax.fori_loop(1, n, finish, 0)

    for bx in range(BPX):
        pieces = []
        for by in range(BPY):
            b = bx * BPY + by
            rank = jnp.int32(0)
            for e in range(b):
                rank = rank + jnp.where(holder[e, 0] == holder[b, 0], 1 - marker[e], 0)
            sea = (1 - marker[b]).astype(jnp.float32)
            pieces.append(got[holder[b, 0], jnp.minimum(rank, CAP - 1)] * sea)
        parts = [swap_groups([piece[f] for piece in pieces]) for f in range(BACK)]
        for q in range(4):
            place = pl.ds(BS * bx + q, 8, stride=4)
            bottom_flux, top_flux, dim, warm, snow, floe, energy = [part[q] for part in parts]
            visible, snowfall, salt = cond[3, place, :], cond[6, place, :], cond[1, place, :]
            out[0, place, :] = bottom_flux
            out[1, place, :] = top_flux
            out[2, place, :] = 0.7 * visible * jnp.exp(-1.5 * snowfall) * dim
            out[3, place, :] = warm
            out[4, place, :] = snow
            out[5, place, :] = floe - 0.05 * bottom_flux
            out[6, place, :] = energy
            out[7, place, :] = -0.05 * bottom_flux * salt


def local(
    interface_conditions, level_warmth_profile, class_coverage_share, class_floe_depth,
    class_drift_depth, floe_drift_speed, internal_tension_tensor, external_drive,
    floe_weight, floe_pressure, holder_lookup, ground_tile_marker,
):
    n, m = lax.axis_size("gy"), lax.axis_size("gx")
    f32 = jnp.float32
    vmem = pl.BlockSpec(memory_space=pltpu.VMEM)
    smem = pl.BlockSpec(memory_space=pltpu.SMEM)
    hbm = pl.BlockSpec(memory_space=pl.ANY)
    shape = jax.ShapeDtypeStruct
    dma = pltpu.SemaphoreType.DMA
    slots, velocity, stress = pl.pallas_call(
        functools.partial(forward_kernel, n, m),
        out_shape=(
            shape((n, CAP, SENT, 8, TILE), f32),
            shape(floe_drift_speed.shape, f32),
            shape(internal_tension_tensor.shape, f32),
        ),
        in_specs=[vmem] * 6 + [smem] * 2,
        out_specs=(vmem,) * 3,
        scratch_shapes=[
            pltpu.VMEM((B, SENT, 8, TILE), f32),
            pltpu.VMEM((n, CAP, SENT, 8, TILE), f32),
            pltpu.VMEM((EVP, ROWS, 2 * TILE), f32),
            pltpu.VMEM((TILE, TILE), f32),
            pltpu.VMEM((TILE, TILE), f32),
            pltpu.VMEM((EVP, HALO, TILE), f32),
            pltpu.VMEM((EVP, HALO, TILE), f32),
            pltpu.VMEM((TILE + 2 * HALO, TILE), f32),
            pltpu.VMEM((TILE + 2 * HALO, TILE), f32),
            pltpu.VMEM((EVP, HALO, TILE), f32),
            pltpu.VMEM((EVP, HALO, TILE), f32),
            dma((n,)), dma((n,)), dma((8,)), dma((8,)),
        ],
        compiler_params=pltpu.CompilerParams(
            collective_id=0, has_side_effects=True, vmem_limit_bytes=VMEM_LIMIT
        ),
    )(
        interface_conditions, floe_drift_speed, internal_tension_tensor, external_drive,
        floe_weight, floe_pressure, holder_lookup, ground_tile_marker,
    )
    warmth, fluxes = pl.pallas_call(
        functools.partial(column_kernel, n),
        out_shape=(
            shape(level_warmth_profile.shape, f32),
            shape((n, CAP, BACK, 8, TILE), f32),
        ),
        in_specs=[vmem] + [hbm] * 4,
        out_specs=(hbm, vmem),
        scratch_shapes=[
            pltpu.VMEM((n * CAP * CLASSES * 8 * 16, TILE), f32),
            pltpu.VMEM((3 * n * CAP * 8 * 8, TILE), f32),
            dma((n, 8)), dma((n, 8)), dma((3, 8)),
        ],
        compiler_params=pltpu.CompilerParams(vmem_limit_bytes=VMEM_LIMIT),
    )(slots, level_warmth_profile, class_coverage_share, class_floe_depth, class_drift_depth)
    exchanges = pl.pallas_call(
        functools.partial(return_kernel, n),
        out_shape=shape(interface_conditions.shape, f32),
        in_specs=[vmem] * 2 + [smem] * 2,
        out_specs=vmem,
        scratch_shapes=[
            pltpu.VMEM((n, CAP, BACK, 8, TILE), f32),
            dma((n,)), dma((n,)),
        ],
        compiler_params=pltpu.CompilerParams(
            collective_id=1, has_side_effects=True, vmem_limit_bytes=VMEM_LIMIT
        ),
    )(fluxes, interface_conditions, holder_lookup, ground_tile_marker)
    return warmth, exchanges, velocity, stress


def solution(mesh):
    tile = P(None, "gx", "gy")
    owner = ("gx", "gy")
    return jax.shard_map(
        local,
        mesh=mesh,
        in_specs=(
            tile, P(owner, None, None, None), P(owner, None, None), P(owner, None, None),
            P(owner, None, None), tile, tile, tile, P("gx", "gy"), P("gx", "gy"),
            P(owner, None), P(owner),
        ),
        out_specs=(P(owner, None, None, None), tile, tile, tile),
        check_vma=False,
    )
```

```python
import functools

import jax
import jax.numpy as jnp
from jax import lax
from jax.experimental import pallas as pl
from jax.experimental.pallas import tpu as pltpu
from jax.sharding import PartitionSpec as P

MESH = pl.DeviceIdType.MESH
BS = 32
BPX = 4
BPY = 4
CAP = 2
ICE = 7
SNOW = 3
LAYERS = 10
CLASSES = 5
SUB = 4
B = 16
TILE = 128
SENT = 6
BACK = 5
EARLY = 2
EVP = 10
HALO = 8
ROWS = TILE + 4 * HALO
VMEM_LIMIT = 62 * 1024 * 1024


def rcp(x):
    r = pl.reciprocal(x, approx=True)
    return r * (2.0 - x * r)


def swap_groups(x):
    group = lax.broadcasted_iota(jnp.int32, x[0].shape, 1) // BS
    even = (group % 2) == 0
    low = group < 2
    y = [None] * 4
    for a in (0, 2):
        y[a] = jnp.where(even, x[a], pltpu.roll(x[a + 1], BS, 1))
        y[a + 1] = jnp.where(even, pltpu.roll(x[a], TILE - BS, 1), x[a + 1])
    z = [None] * 4
    for a in (0, 1):
        z[a] = jnp.where(low, y[a], pltpu.roll(y[a + 2], 2 * BS, 1))
        z[a + 2] = jnp.where(low, pltpu.roll(y[a], 2 * BS, 1), y[a + 2])
    return z


def evp_steps(ext):
    bands = [2 * HALO * i + HALO for i in range((TILE + 2 * HALO) // (2 * HALO))]
    size = 2 * HALO
    third = 1.0 / 1.5

    def d_row(f, r):
        return 0.5 * (ext[f, r + 1 : r + 1 + size, :] - ext[f, r - 1 : r - 1 + size, :])

    def d_lane(x):
        width = x.shape[1]
        return 0.5 * (pltpu.roll(x, width - 1, 1) - pltpu.roll(x, 1, 1))

    def step(_, carry):
        for r in bands:
            here = slice(r, r + size)
            ux, uy = d_row(0, r), d_lane(ext[0, here, :])
            vx, vy = d_row(1, r), d_lane(ext[1, here, :])
            diverge, tension, shearing = ux + vy, ux - vy, uy + vx
            square = diverge * diverge + 0.25 * (tension * tension + shearing * shearing) + 0.04
            inverse = lax.rsqrt(square)
            push = ext[9, here, :]
            scaled = push * inverse
            ext[2, here, :] = third * ext[2, here, :] + (scaled * diverge - push)
            ext[3, here, :] = third * ext[3, here, :] + 0.25 * (scaled * tension)
            ext[4, here, :] = third * ext[4, here, :] + 0.125 * (scaled * shearing)
        for r in bands:
            here = slice(r, r + size)
            force_x = 0.5 * (d_row(2, r) + d_row(3, r)) + d_lane(ext[4, here, :])
            force_y = 0.5 * d_lane(ext[2, here, :] - ext[3, here, :]) + d_row(4, r)
            east, north = ext[0, here, :], ext[1, here, :]
            half, keep = ext[5, here, :], ext[6, here, :]
            ext[0, here, :] = keep * (east + 0.15 * north) + half * force_x + ext[7, here, :]
            ext[1, here, :] = keep * (north - 0.15 * east) + half * force_y + ext[8, here, :]
        return carry

    lax.fori_loop(0, SUB, step, 0)


def parcels(n, gx, gy, rows, src, dst, send_sem, recv_sem):
    def sending(o):
        return pltpu.make_async_remote_copy(
            src_ref=src.at[pl.ds(o * rows, rows)], dst_ref=dst.at[pl.ds(gy * rows, rows)],
            send_sem=send_sem.at[o], recv_sem=recv_sem.at[gy],
            device_id=(gx, o), device_id_type=MESH,
        )

    def arriving(t):
        return pltpu.make_async_remote_copy(
            src_ref=src.at[pl.ds(t * rows, rows)], dst_ref=dst.at[pl.ds(t * rows, rows)],
            send_sem=send_sem.at[t], recv_sem=recv_sem.at[t],
            device_id=(gx, t), device_id_type=MESH,
        )

    return sending, arriving


def main_kernel(
    n, m,
    cond_far, vel_far, stress_far, drive_far, weight_far, pressure_far, holder, marker,
    warmth_far, share_far, thick_far, drift_far,
    new_far, got, got_early, coef, vel_out, stress_out,
    held, cond, vel, stress, drive, weight, pressure, share, thick, drift,
    blk, send, slots, early, fluxes,
    ext, pack_w, pack_e, top, bottom, got_w, got_e, got_t, got_b,
    in_sem, warm_sem, new_sem, send_sem, recv_sem, esend_sem, erecv_sem, fsend_sem, frecv_sem,
    hsend_sem, hrecv_sem,
):
    gx, gy = lax.axis_index("gx"), lax.axis_index("gy")
    up, down = lax.rem(gx + m - 1, m), lax.rem(gx + 1, m)
    left, right = lax.rem(gy + n - 1, n), lax.rem(gy + 1, n)
    around = [(up, gy), (down, gy), (up, left), (up, right), (down, left), (down, right)]
    groups = n * CAP // 8
    per_group = 8 // CAP
    reach = sorted(range(1, n), key=lambda k: abs(k - n // 2))

    pairs = (
        (cond_far, cond), (share_far, share), (thick_far, thick), (drift_far, drift),
        (vel_far, vel), (stress_far, stress), (drive_far, drive),
        (weight_far, weight), (pressure_far, pressure),
    )
    loads = [pltpu.make_async_copy(a, b, in_sem.at[i]) for i, (a, b) in enumerate(pairs)]

    def warm_load(g):
        at = pl.ds(pl.multiple_of(8 * g, 8), 8)
        return pltpu.make_async_copy(
            warmth_far.at[:, :, at, :], held.at[:, :, at, :], warm_sem.at[g]
        )

    def new_store(g):
        at = pl.ds(pl.multiple_of(8 * g, 8), 8)
        return pltpu.make_async_copy(
            held.at[:, :, at, :], new_far.at[:, :, at, :], new_sem.at[g]
        )

    loads[0].start()
    barrier = pltpu.get_barrier_semaphore()
    for k in reach:
        pl.semaphore_signal(
            barrier, inc=1, device_id=(gx, lax.rem(gy + k, n)), device_id_type=MESH
        )
    for device in around:
        pl.semaphore_signal(barrier, inc=1, device_id=device, device_id_type=MESH)
    for copy in loads[1:]:
        copy.start()
    for g in range(groups):
        warm_load(g).start()

    loads[0].wait()
    for bx in range(BPX):
        def part(f, q):
            return cond[f, pl.ds(BS * bx + q, 8, stride=4), :]

        for at, f in enumerate((0, 1, 2, None, 6, 7)):
            if f is None:
                pieces = [
                    0.25 * part(3, q) + 0.45 * part(4, q) + 0.3 * part(5, q) for q in range(4)
                ]
            else:
                pieces = [part(f, q) for q in range(4)]
            for by, piece in enumerate(swap_groups(pieces)):
                blk[bx * BPY + by, 8 * at : 8 * at + 8, :] = piece

    block_rows = SENT * 8

    def fill(o, carry):
        count = jnp.int32(0)
        first = jnp.int32(0)
        second = jnp.int32(0)
        for b in range(B):
            hit = jnp.where(holder[b] == o, 1 - marker[b], 0)
            first = first + jnp.where(count == 0, hit * b, 0)
            second = second + jnp.where(count == 1, hit * b, 0)
            count = count + hit
        has_first = jnp.where(count > 0, 1.0, 0.0)
        has_second = jnp.where(count > 1, 1.0, 0.0)
        at = pl.multiple_of(o * (CAP * block_rows), 8)
        send[pl.ds(at, block_rows), :] = blk[first] * has_first
        send[pl.ds(pl.multiple_of(at + block_rows, 8), block_rows), :] = blk[second] * has_second
        return carry

    lax.fori_loop(0, n, fill, 0)

    pl.semaphore_wait(barrier, n - 1 + len(around))

    sending, arriving = parcels(
        n, gx, gy, CAP * block_rows, send, slots, send_sem, recv_sem
    )
    for k in reach:
        sending(lax.rem(gy + k, n)).start()
    mine = pl.ds(pl.multiple_of(gy * (CAP * block_rows), 8), CAP * block_rows)
    slots[mine, :] = send[mine, :]

    for copy in loads[1:4]:
        copy.wait()

    def ahead(i, carry):
        g, j = i // 8, lax.rem(i, 8)
        at = pl.ds(pl.multiple_of(8 * g, 8), 8)
        cells = pl.ds(pl.multiple_of(TILE * j, TILE), TILE)
        dim = jnp.zeros((8, TILE), jnp.float32)
        floe = jnp.zeros((8, TILE), jnp.float32)
        for c in range(CLASSES):
            area, deep = share[c, at, cells], thick[c, at, cells]
            dim = dim + area * jnp.exp(-5.0 * drift[c, at, cells] - 1.5 * deep)
            floe = floe + area * deep
        early[pl.ds(g * (8 * 16) + j, 8, stride=16), :] = dim
        early[pl.ds(g * (8 * 16) + 8 + j, 8, stride=16), :] = floe
        return carry

    lax.fori_loop(0, groups * 8, ahead, 0)
    esending, earriving = parcels(
        n, gx, gy, CAP * EARLY * 8, early, got_early, esend_sem, erecv_sem
    )
    for k in reach:
        esending(lax.rem(gy + k, n)).start()
    mine_early = pl.ds(pl.multiple_of(gy * (CAP * EARLY * 8), 8), CAP * EARLY * 8)
    got_early[mine_early, :] = early[mine_early, :]

    for copy in loads[4:]:
        copy.wait()
    inner = slice(2 * HALO, 2 * HALO + TILE)
    ext[...] = jnp.zeros_like(ext)
    for f in range(2):
        ext[f, inner, :TILE] = vel[f]
    for f in range(3):
        ext[2 + f, inner, :TILE] = stress[f]
    column = lax.broadcasted_iota(jnp.int32, (BS, TILE), 1) // BS
    for bx in range(BPX):
        rows = slice(BS * bx, BS * bx + BS)
        into = slice(2 * HALO + BS * bx, 2 * HALO + BS * bx + BS)
        water = jnp.zeros((BS, TILE), jnp.float32)
        for by in range(BPY):
            sea = (1 - marker[bx * BPY + by]).astype(jnp.float32)
            water = jnp.where(column == by, sea, water)
        w = weight[rows, :]
        open_part = water * rcp(w + 0.5)
        half = 0.5 * open_part
        ext[5, into, :TILE] = half
        ext[6, into, :TILE] = open_part * w
        ext[7, into, :TILE] = half * (drive[0, rows, :] + drive[2, rows, :])
        ext[8, into, :TILE] = half * (drive[1, rows, :] + drive[3, rows, :])
        ext[9, into, :TILE] = pressure[rows, :] * (1.0 / 3.0)

    lane = lax.broadcasted_iota(jnp.int32, (TILE, TILE), 1)
    packed_w = jnp.zeros((TILE, TILE), jnp.float32)
    packed_e = jnp.zeros((TILE, TILE), jnp.float32)
    for f in range(EVP):
        own = (lane // HALO) == f
        x = ext[f, inner, :TILE]
        packed_w = jnp.where(own, pltpu.roll(x, HALO * f, 1) if f else x, packed_w)
        packed_e = jnp.where(own, pltpu.roll(x, HALO * (f + 1), 1), packed_e)
        top[f] = ext[f, 2 * HALO : 3 * HALO, :TILE]
        bottom[f] = ext[f, HALO + TILE : 2 * HALO + TILE, :TILE]
    pack_w[...] = packed_w
    pack_e[...] = packed_e

    head, tail = pl.ds(0, HALO), pl.ds(TILE - HALO, HALO)
    first, middle, last = pl.ds(0, HALO), pl.ds(HALO, TILE), pl.ds(HALO + TILE, HALO)
    halos = [
        (pack_w, got_e.at[middle], (gx, left)),
        (pack_e, got_w.at[middle], (gx, right)),
        (top, got_b, (up, gy)),
        (bottom, got_t, (down, gy)),
        (pack_w.at[head], got_e.at[last], (up, left)),
        (pack_e.at[head], got_w.at[last], (up, right)),
        (pack_w.at[tail], got_e.at[first], (down, left)),
        (pack_e.at[tail], got_w.at[first], (down, right)),
    ]
    copies = [
        pltpu.make_async_remote_copy(
            src_ref=src, dst_ref=dst, send_sem=hsend_sem.at[i], recv_sem=hrecv_sem.at[i],
            device_id=device, device_id_type=MESH,
        )
        for i, (src, dst, device) in enumerate(halos)
    ]
    for copy in copies:
        copy.start()
    coef[0] = 0.7 * cond[3] * jnp.exp(-1.5 * cond[6])
    coef[1] = -0.05 * cond[1]

    fsending, farriving = parcels(n, gx, gy, CAP * BACK * 8, fluxes, got, fsend_sem, frecv_sem)
    own_group = gy // per_group
    for i in range(groups):
        g = lax.rem(own_group + i, groups)
        for e in range(per_group):
            t = g * per_group + e

            @pl.when(t != gy)
            def _():
                arriving(t).wait_recv()

        warm_load(g).wait()

        def chunk(j, carry):
            column_step(g, j, slots, held, share, thick, drift, fluxes)
            return carry

        lax.fori_loop(0, 8, chunk, 0)
        new_store(g).start()
        for e in range(per_group):
            t = g * per_group + e

            @pl.when(t != gy)
            def _():
                fsending(t).start()

    mine_back = pl.ds(pl.multiple_of(gy * (CAP * BACK * 8), 8), CAP * BACK * 8)
    got[mine_back, :] = fluxes[mine_back, :]

    for copy in copies:
        copy.wait()
    on_top = jnp.where(gx > 0, 1.0, 0.0)
    on_bottom = jnp.where(gx < m - 1, 1.0, 0.0)
    on_left = jnp.where(gy > 0, 1.0, 0.0)
    on_right = jnp.where(gy < n - 1, 1.0, 0.0)
    tall = TILE + 2 * HALO
    row = lax.broadcasted_iota(jnp.int32, (tall, TILE), 0)
    lane = lax.broadcasted_iota(jnp.int32, (tall, TILE), 1)
    upright = jnp.where(row < HALO, on_top, jnp.where(row < HALO + TILE, 1.0, on_bottom))
    sided_e = got_e[...] * (upright * on_right)
    sided_w = got_w[...] * (upright * on_left)
    for f in range(EVP):
        ext[f, HALO : 2 * HALO, :TILE] = got_t[f] * on_top
        ext[f, 2 * HALO + TILE : 3 * HALO + TILE, :TILE] = got_b[f] * on_bottom
        from_e = pltpu.roll(sided_e, TILE - HALO * f, 1) if f else sided_e
        from_w = pltpu.roll(sided_w, TILE - HALO * (f + 1), 1)
        ext[f, HALO : HALO + tall, TILE:] = jnp.where(
            lane < HALO, from_e, jnp.where(lane >= TILE - HALO, from_w, 0.0)
        )

    evp_steps(ext)
    for f in range(2):
        vel_out[f] = ext[f, inner, :TILE]
    for f in range(3):
        stress_out[f] = ext[2 + f, inner, :TILE]

    for g in range(groups):
        new_store(g).wait()
    for k in reach:
        o = lax.rem(gy + k, n)
        sending(o).wait_send()
        esending(o).wait_send()
        earriving(o).wait_recv()
        fsending(o).wait_send()
        farriving(o).wait_recv()


def column_step(g, j, slots, held, share, thick, drift, fluxes):
    at = pl.ds(pl.multiple_of(8 * g, 8), 8)
    cells = pl.ds(pl.multiple_of(TILE * j, TILE), TILE)
    ocean, salt, air, source, snowfall, wind = [
        slots[pl.ds(g * (64 * SENT) + 8 * f + j, 8, stride=8 * SENT), :] for f in range(SENT)
    ]
    filled = salt > 0.25
    air_resist = rcp(1.0 + 2.0 * wind)
    sums = None
    for c in range(CLASSES):
        area, floe, lying = share[c, at, cells], thick[c, at, cells], drift[c, at, cells]
        snow = lying + 0.3 * snowfall
        depth = floe * (1.0 / ICE)
        twice = 2.0 * depth
        snow_mass = snow * (2.0 / 3.0)
        snow_resist = snow * (1.0 / 0.9)
        snow_cond = rcp(snow_resist)
        top = rcp(0.5 * snow_resist + air_resist)
        above, resist = top, snow_resist
        ratios, values = [], []
        content = None
        for l in range(LAYERS):
            old = held[c, l, at, cells]
            if l < SNOW:
                mass = snow_mass
            else:
                brine = salt * (0.2 + 0.1 * (l - SNOW))
                mass = twice + twice * (0.2 * brine) * rcp(old * old + 0.1)
            if l < SNOW - 1:
                below = snow_cond
            elif l < LAYERS - 1:
                brine = salt * (0.2 + 0.1 * (l + 1 - SNOW))
                shifted = held[c, l + 1, at, cells] - 0.5
                later = depth * shifted * rcp(2.0 * shifted + 0.1 * brine)
                below = 2.0 * rcp(resist + later)
                resist = later
            else:
                below = 2.0 * rcp(resist)
            held_heat = mass * old
            content = held_heat if content is None else content + held_heat
            carried = held_heat
            pivot = mass + above + below
            if l == 0:
                carried = carried + top * air + source
            if l == LAYERS - 1:
                carried = carried + below * ocean
            if l > 0:
                pivot = pivot - above * ratios[-1]
                carried = carried + above * values[-1]
            inverse = rcp(pivot)
            ratios.append(below * inverse)
            values.append(carried * inverse)
            above = below
        new = values[-1]
        last = new
        held[c, LAYERS - 1, at, cells] = jnp.where(filled, new, held[c, LAYERS - 1, at, cells])
        for l in range(LAYERS - 2, -1, -1):
            new = values[l] + ratios[l] * new
            held[c, l, at, cells] = jnp.where(filled, new, held[c, l, at, cells])
        bottom_flux = below * (last - ocean)
        top_flux = top * (air - new)
        terms = [
            bottom_flux, top_flux, new, snow,
            0.05 * (content + top_flux - bottom_flux + source),
        ]
        terms = [area * term for term in terms]
        sums = terms if sums is None else [a + b for a, b in zip(sums, terms)]
    for f in range(BACK):
        fluxes[pl.ds(g * (64 * BACK) + 8 * f + j, 8, stride=8 * BACK), :] = sums[f]


def output_kernel(
    n, held, got, got_early, coef, vel, stress, holder, marker,
    warmth_far, out_far, vel_far, stress_far, out, sem,
):
    copies = [
        pltpu.make_async_copy(a, b, sem.at[i])
        for i, (a, b) in enumerate(((held, warmth_far), (vel, vel_far), (stress, stress_far)))
    ]
    for copy in copies:
        copy.start()
    rows_back, rows_early = 8 * BACK, 8 * EARLY
    for bx in range(BPX):
        pieces = []
        for by in range(BPY):
            b = bx * BPY + by
            rank = jnp.int32(0)
            for e in range(b):
                rank = rank + jnp.where(holder[e] == holder[b], 1 - marker[e], 0)
            sea = (1 - marker[b]).astype(jnp.float32)
            s = holder[b] * CAP + jnp.minimum(rank, CAP - 1)
            one = [got[pl.ds(pl.multiple_of(s * rows_back + 8 * f, 8), 8), :] for f in range(BACK)]
            two = [
                got_early[pl.ds(pl.multiple_of(s * rows_early + 8 * f, 8), 8), :]
                for f in range(EARLY)
            ]
            pieces.append([x * sea for x in one + two])
        parts = [swap_groups([piece[f] for piece in pieces]) for f in range(BACK + EARLY)]
        for q in range(4):
            place = pl.ds(BS * bx + q, 8, stride=4)
            bottom_flux, top_flux, warm, snow, energy, dim, floe = [part[q] for part in parts]
            out[0, place, :] = bottom_flux
            out[1, place, :] = top_flux
            out[2, place, :] = coef[0, place, :] * dim
            out[3, place, :] = warm
            out[4, place, :] = snow
            out[5, place, :] = floe - 0.05 * bottom_flux
            out[6, place, :] = energy
            out[7, place, :] = coef[1, place, :] * bottom_flux
    last = pltpu.make_async_copy(out, out_far, sem.at[len(copies)])
    last.start()
    for copy in copies:
        copy.wait()
    last.wait()


def local(
    interface_conditions, level_warmth_profile, class_coverage_share, class_floe_depth,
    class_drift_depth, floe_drift_speed, internal_tension_tensor, external_drive,
    floe_weight, floe_pressure, holder_lookup, ground_tile_marker,
):
    n, m = lax.axis_size("gy"), lax.axis_size("gx")
    f32 = jnp.float32
    vmem = pl.BlockSpec(memory_space=pltpu.VMEM)
    smem = pl.BlockSpec(memory_space=pltpu.SMEM)
    hbm = pl.BlockSpec(memory_space=pltpu.HBM)
    shape = jax.ShapeDtypeStruct
    dma = pltpu.SemaphoreType.DMA
    holder = holder_lookup.reshape(-1)
    warmth = jnp.transpose(level_warmth_profile, (1, 2, 0, 3))
    share, thick, drift = [
        jnp.transpose(x, (1, 0, 2))
        for x in (class_coverage_share, class_floe_depth, class_drift_depth)
    ]
    places = n * CAP
    like = lambda x: pltpu.VMEM(x.shape, f32)
    held, got, got_early, coef, velocity, stress = pl.pallas_call(
        functools.partial(main_kernel, n, m),
        out_shape=(
            shape(warmth.shape, f32),
            shape((places * BACK * 8, TILE), f32),
            shape((places * EARLY * 8, TILE), f32),
            shape((2, TILE, TILE), f32),
            shape(floe_drift_speed.shape, f32),
            shape(internal_tension_tensor.shape, f32),
        ),
        in_specs=[hbm] * 6 + [smem] * 2 + [hbm] * 4,
        out_specs=(hbm,) + (vmem,) * 5,
        scratch_shapes=[
            like(warmth),
            like(interface_conditions), like(floe_drift_speed), like(internal_tension_tensor),
            like(external_drive), like(floe_weight), like(floe_pressure),
            like(share), like(thick), like(drift),
            pltpu.VMEM((B, SENT * 8, TILE), f32),
            pltpu.VMEM((places * SENT * 8, TILE), f32),
            pltpu.VMEM((places * SENT * 8, TILE), f32),
            pltpu.VMEM((places * EARLY * 8, TILE), f32),
            pltpu.VMEM((places * BACK * 8, TILE), f32),
            pltpu.VMEM((EVP, ROWS, 2 * TILE), f32),
            pltpu.VMEM((TILE, TILE), f32),
            pltpu.VMEM((TILE, TILE), f32),
            pltpu.VMEM((EVP, HALO, TILE), f32),
            pltpu.VMEM((EVP, HALO, TILE), f32),
            pltpu.VMEM((TILE + 2 * HALO, TILE), f32),
            pltpu.VMEM((TILE + 2 * HALO, TILE), f32),
            pltpu.VMEM((EVP, HALO, TILE), f32),
            pltpu.VMEM((EVP, HALO, TILE), f32),
            dma((9,)), dma((places // 8,)), dma((places // 8,)),
            dma((n,)), dma((n,)), dma((n,)), dma((n,)), dma((n,)), dma((n,)),
            dma((8,)), dma((8,)),
        ],
        compiler_params=pltpu.CompilerParams(
            collective_id=0, has_side_effects=True, vmem_limit_bytes=VMEM_LIMIT
        ),
    )(
        interface_conditions, floe_drift_speed, internal_tension_tensor, external_drive,
        floe_weight, floe_pressure, holder, ground_tile_marker, warmth, share, thick, drift,
    )
    warmth, exchanges, velocity, stress = pl.pallas_call(
        functools.partial(output_kernel, n),
        out_shape=tuple(
            shape(x.shape, f32) for x in (held, interface_conditions, velocity, stress)
        ),
        in_specs=[hbm] + [vmem] * 3 + [hbm] * 2 + [smem] * 2,
        out_specs=(hbm,) * 4,
        scratch_shapes=[like(interface_conditions), dma((4,))],
        compiler_params=pltpu.CompilerParams(vmem_limit_bytes=VMEM_LIMIT),
    )(held, got, got_early, coef, velocity, stress, holder, ground_tile_marker)
    return jnp.transpose(warmth, (2, 0, 1, 3)), exchanges, velocity, stress


def solution(mesh):
    tile = P(None, "gx", "gy")
    owner = ("gx", "gy")
    return jax.shard_map(
        local,
        mesh=mesh,
        in_specs=(
            tile, P(owner, None, None, None), P(owner, None, None), P(owner, None, None),
            P(owner, None, None), tile, tile, tile, P("gx", "gy"), P("gx", "gy"),
            P(owner, None), P(owner),
        ),
        out_specs=(P(owner, None, None, None), tile, tile, tile),
        check_vma=False,
    )
```

```python
import functools

import jax
import jax.numpy as jnp
from jax import lax
from jax.experimental import pallas as pl
from jax.experimental.pallas import tpu as pltpu
from jax.sharding import PartitionSpec as P

MESH = pl.DeviceIdType.MESH
BS = 32
BPX = 4
BPY = 4
CAP = 2
ICE = 7
SNOW = 3
LAYERS = 10
CLASSES = 5
SUB = 4
B = 16
TILE = 128
SENT = 6
BACK = 5
EARLY = 2
EVP = 10
HALO = 8
ROWS = TILE + 4 * HALO
VMEM_LIMIT = 62 * 1024 * 1024


def rcp(x):
    r = pl.reciprocal(x, approx=True)
    return r * (2.0 - x * r)


def swap_groups(x):
    group = lax.broadcasted_iota(jnp.int32, x[0].shape, 1) // BS
    even = (group % 2) == 0
    low = group < 2
    y = [None] * 4
    for a in (0, 2):
        y[a] = jnp.where(even, x[a], pltpu.roll(x[a + 1], BS, 1))
        y[a + 1] = jnp.where(even, pltpu.roll(x[a], TILE - BS, 1), x[a + 1])
    z = [None] * 4
    for a in (0, 1):
        z[a] = jnp.where(low, y[a], pltpu.roll(y[a + 2], 2 * BS, 1))
        z[a + 2] = jnp.where(low, pltpu.roll(y[a], 2 * BS, 1), y[a + 2])
    return z


def evp_steps(ext):
    bands = [2 * HALO * i + HALO for i in range((TILE + 2 * HALO) // (2 * HALO))]
    size = 2 * HALO
    third = 1.0 / 1.5

    def d_row(f, r):
        return 0.5 * (ext[f, r + 1 : r + 1 + size, :] - ext[f, r - 1 : r - 1 + size, :])

    def d_lane(x):
        width = x.shape[1]
        return 0.5 * (pltpu.roll(x, width - 1, 1) - pltpu.roll(x, 1, 1))

    def step(_, carry):
        for r in bands:
            here = slice(r, r + size)
            ux, uy = d_row(0, r), d_lane(ext[0, here, :])
            vx, vy = d_row(1, r), d_lane(ext[1, here, :])
            diverge, tension, shearing = ux + vy, ux - vy, uy + vx
            square = diverge * diverge + 0.25 * (tension * tension + shearing * shearing) + 0.04
            inverse = lax.rsqrt(square)
            push = ext[9, here, :]
            scaled = push * inverse
            ext[2, here, :] = third * ext[2, here, :] + (scaled * diverge - push)
            ext[3, here, :] = third * ext[3, here, :] + 0.25 * (scaled * tension)
            ext[4, here, :] = third * ext[4, here, :] + 0.125 * (scaled * shearing)
        for r in bands:
            here = slice(r, r + size)
            force_x = 0.5 * (d_row(2, r) + d_row(3, r)) + d_lane(ext[4, here, :])
            force_y = 0.5 * d_lane(ext[2, here, :] - ext[3, here, :]) + d_row(4, r)
            east, north = ext[0, here, :], ext[1, here, :]
            half, keep = ext[5, here, :], ext[6, here, :]
            ext[0, here, :] = keep * (east + 0.15 * north) + half * force_x + ext[7, here, :]
            ext[1, here, :] = keep * (north - 0.15 * east) + half * force_y + ext[8, here, :]
        return carry

    lax.fori_loop(0, SUB, step, 0)


def parcels(n, gx, gy, rows, src, dst, send_sem, recv_sem):
    def sending(o):
        return pltpu.make_async_remote_copy(
            src_ref=src.at[pl.ds(o * rows, rows)], dst_ref=dst.at[pl.ds(gy * rows, rows)],
            send_sem=send_sem.at[o], recv_sem=recv_sem.at[gy],
            device_id=(gx, o), device_id_type=MESH,
        )

    def arriving(t):
        return pltpu.make_async_remote_copy(
            src_ref=src.at[pl.ds(t * rows, rows)], dst_ref=dst.at[pl.ds(t * rows, rows)],
            send_sem=send_sem.at[t], recv_sem=recv_sem.at[t],
            device_id=(gx, t), device_id_type=MESH,
        )

    return sending, arriving


def main_kernel(
    n, m,
    cond_far, vel_far, stress_far, drive_far, weight_far, pressure_far, holder, marker,
    warmth_far, share_far, thick_far, drift_far,
    new_far, got_far, early_far, coef_far, vel_out, stress_out,
    held, got, got_early, coef, picks, cond, vel, stress, drive, weight, pressure, share, thick, drift,
    blk, send, slots, early, fluxes,
    ext, pack_w, pack_e, top, bottom, got_w, got_e, got_t, got_b,
    in_sem, warm_sem, new_sem, out_sem, send_sem, recv_sem, esend_sem, erecv_sem, fsend_sem, frecv_sem,
    hsend_sem, hrecv_sem,
):
    gx, gy = lax.axis_index("gx"), lax.axis_index("gy")
    up, down = lax.rem(gx + m - 1, m), lax.rem(gx + 1, m)
    left, right = lax.rem(gy + n - 1, n), lax.rem(gy + 1, n)
    around = [(up, gy), (down, gy), (up, left), (up, right), (down, left), (down, right)]
    groups = n * CAP // 8
    per_group = 8 // CAP
    reach = sorted(range(1, n), key=lambda k: abs(k - n // 2))

    pairs = (
        (cond_far, cond), (share_far, share), (thick_far, thick), (drift_far, drift),
        (vel_far, vel), (stress_far, stress), (drive_far, drive),
        (weight_far, weight), (pressure_far, pressure),
    )
    loads = [pltpu.make_async_copy(a, b, in_sem.at[i]) for i, (a, b) in enumerate(pairs)]

    def warm_load(g):
        at = pl.ds(pl.multiple_of(8 * g, 8), 8)
        return pltpu.make_async_copy(
            warmth_far.at[:, :, at, :], held.at[:, :, at, :], warm_sem.at[g]
        )

    def new_store(g):
        at = pl.ds(pl.multiple_of(8 * g, 8), 8)
        return pltpu.make_async_copy(
            held.at[:, :, at, :], new_far.at[:, :, at, :], new_sem.at[g]
        )

    loads[0].start()
    barrier = pltpu.get_barrier_semaphore()
    for k in reach:
        pl.semaphore_signal(
            barrier, inc=1, device_id=(gx, lax.rem(gy + k, n)), device_id_type=MESH
        )
    for device in around:
        pl.semaphore_signal(barrier, inc=1, device_id=device, device_id_type=MESH)
    for copy in loads[1:]:
        copy.start()
    for g in range(groups):
        warm_load(g).start()

    def find(o, carry):
        count = jnp.int32(0)
        first = jnp.int32(0)
        second = jnp.int32(0)
        for b in range(B):
            hit = jnp.where(holder[b] == o, 1 - marker[b], 0)
            first = first + jnp.where(count == 0, hit * b, 0)
            second = second + jnp.where(count == 1, hit * b, 0)
            count = count + hit
        picks[0, o] = first
        picks[1, o] = second
        picks[2, o] = count
        return carry

    lax.fori_loop(0, n, find, 0)
    loads[0].wait()
    for bx in range(BPX):
        def part(f, q):
            return cond[f, pl.ds(BS * bx + q, 8, stride=4), :]

        for at, f in enumerate((0, 1, 2, None, 6, 7)):
            if f is None:
                pieces = [
                    0.25 * part(3, q) + 0.45 * part(4, q) + 0.3 * part(5, q) for q in range(4)
                ]
            else:
                pieces = [part(f, q) for q in range(4)]
            for by, piece in enumerate(swap_groups(pieces)):
                blk[bx * BPY + by, 8 * at : 8 * at + 8, :] = piece

    block_rows = SENT * 8

    def fill(o, carry):
        first, second, count = picks[0, o], picks[1, o], picks[2, o]
        has_first = jnp.where(count > 0, 1.0, 0.0)
        has_second = jnp.where(count > 1, 1.0, 0.0)
        at = pl.multiple_of(o * (CAP * block_rows), 8)
        send[pl.ds(at, block_rows), :] = blk[first] * has_first
        send[pl.ds(pl.multiple_of(at + block_rows, 8), block_rows), :] = blk[second] * has_second
        return carry

    lax.fori_loop(0, n, fill, 0)

    pl.semaphore_wait(barrier, n - 1 + len(around))

    sending, arriving = parcels(
        n, gx, gy, CAP * block_rows, send, slots, send_sem, recv_sem
    )
    for k in reach:
        sending(lax.rem(gy + k, n)).start()
    mine = pl.ds(pl.multiple_of(gy * (CAP * block_rows), 8), CAP * block_rows)
    slots[mine, :] = send[mine, :]

    for copy in loads[1:4]:
        copy.wait()

    def ahead(i, carry):
        g, j = i // 8, lax.rem(i, 8)
        at = pl.ds(pl.multiple_of(8 * g, 8), 8)
        cells = pl.ds(pl.multiple_of(TILE * j, TILE), TILE)
        dim = jnp.zeros((8, TILE), jnp.float32)
        floe = jnp.zeros((8, TILE), jnp.float32)
        for c in range(CLASSES):
            area, deep = share[c, at, cells], thick[c, at, cells]
            dim = dim + area * jnp.exp(-5.0 * drift[c, at, cells] - 1.5 * deep)
            floe = floe + area * deep
        early[pl.ds(g * (8 * 16) + j, 8, stride=16), :] = dim
        early[pl.ds(g * (8 * 16) + 8 + j, 8, stride=16), :] = floe
        return carry

    lax.fori_loop(0, groups * 8, ahead, 0)
    esending, earriving = parcels(
        n, gx, gy, CAP * EARLY * 8, early, got_early, esend_sem, erecv_sem
    )
    for k in reach:
        esending(lax.rem(gy + k, n)).start()
    mine_early = pl.ds(pl.multiple_of(gy * (CAP * EARLY * 8), 8), CAP * EARLY * 8)
    got_early[mine_early, :] = early[mine_early, :]

    for copy in loads[4:]:
        copy.wait()
    inner = slice(2 * HALO, 2 * HALO + TILE)
    ext[...] = jnp.zeros_like(ext)
    for f in range(2):
        ext[f, inner, :TILE] = vel[f]
    for f in range(3):
        ext[2 + f, inner, :TILE] = stress[f]
    column = lax.broadcasted_iota(jnp.int32, (BS, TILE), 1) // BS
    for bx in range(BPX):
        rows = slice(BS * bx, BS * bx + BS)
        into = slice(2 * HALO + BS * bx, 2 * HALO + BS * bx + BS)
        water = jnp.zeros((BS, TILE), jnp.float32)
        for by in range(BPY):
            sea = (1 - marker[bx * BPY + by]).astype(jnp.float32)
            water = jnp.where(column == by, sea, water)
        w = weight[rows, :]
        open_part = water * rcp(w + 0.5)
        half = 0.5 * open_part
        ext[5, into, :TILE] = half
        ext[6, into, :TILE] = open_part * w
        ext[7, into, :TILE] = half * (drive[0, rows, :] + drive[2, rows, :])
        ext[8, into, :TILE] = half * (drive[1, rows, :] + drive[3, rows, :])
        ext[9, into, :TILE] = pressure[rows, :] * (1.0 / 3.0)

    lane = lax.broadcasted_iota(jnp.int32, (TILE, TILE), 1)
    packed_w = jnp.zeros((TILE, TILE), jnp.float32)
    packed_e = jnp.zeros((TILE, TILE), jnp.float32)
    for f in range(EVP):
        own = (lane // HALO) == f
        x = ext[f, inner, :TILE]
        packed_w = jnp.where(own, pltpu.roll(x, HALO * f, 1) if f else x, packed_w)
        packed_e = jnp.where(own, pltpu.roll(x, HALO * (f + 1), 1), packed_e)
        top[f] = ext[f, 2 * HALO : 3 * HALO, :TILE]
        bottom[f] = ext[f, HALO + TILE : 2 * HALO + TILE, :TILE]
    pack_w[...] = packed_w
    pack_e[...] = packed_e

    head, tail = pl.ds(0, HALO), pl.ds(TILE - HALO, HALO)
    first, middle, last = pl.ds(0, HALO), pl.ds(HALO, TILE), pl.ds(HALO + TILE, HALO)
    has_up, has_down, has_left, has_right = gx > 0, gx < m - 1, gy > 0, gy < n - 1
    both = jnp.logical_and
    halos = [
        (pack_w, got_e.at[middle], (gx, left), has_left, has_right),
        (pack_e, got_w.at[middle], (gx, right), has_right, has_left),
        (top, got_b, (up, gy), has_up, has_down),
        (bottom, got_t, (down, gy), has_down, has_up),
        (pack_w.at[head], got_e.at[last], (up, left), both(has_up, has_left),
         both(has_down, has_right)),
        (pack_e.at[head], got_w.at[last], (up, right), both(has_up, has_right),
         both(has_down, has_left)),
        (pack_w.at[tail], got_e.at[first], (down, left), both(has_down, has_left),
         both(has_up, has_right)),
        (pack_e.at[tail], got_w.at[first], (down, right), both(has_down, has_right),
         both(has_up, has_left)),
    ]

    def halo(i):
        src, dst, device = halos[i][:3]
        return pltpu.make_async_remote_copy(
            src_ref=src, dst_ref=dst, send_sem=hsend_sem.at[i], recv_sem=hrecv_sem.at[i],
            device_id=device, device_id_type=MESH,
        )

    for i in range(len(halos)):
        @pl.when(halos[i][3])
        def _():
            halo(i).start()
    coef[0] = 0.7 * cond[3] * jnp.exp(-1.5 * cond[6])
    coef[1] = -0.05 * cond[1]
    results = ((coef, coef_far), (vel, vel_out), (stress, stress_out), (got_early, early_far), (got, got_far))
    stores = [pltpu.make_async_copy(a, b, out_sem.at[i]) for i, (a, b) in enumerate(results)]
    stores[0].start()

    fsending, farriving = parcels(n, gx, gy, CAP * BACK * 8, fluxes, got, fsend_sem, frecv_sem)
    own_group = gy // per_group
    for i in range(groups):
        g = lax.rem(own_group + i, groups)
        for e in range(per_group):
            t = g * per_group + e

            @pl.when(t != gy)
            def _():
                arriving(t).wait_recv()

        warm_load(g).wait()

        def chunk(j, carry):
            column_step(g, j, slots, held, share, thick, drift, fluxes)
            return carry

        lax.fori_loop(0, 8, chunk, 0)
        new_store(g).start()
        for e in range(per_group):
            t = g * per_group + e

            @pl.when(t != gy)
            def _():
                fsending(t).start()

    mine_back = pl.ds(pl.multiple_of(gy * (CAP * BACK * 8), 8), CAP * BACK * 8)
    got[mine_back, :] = fluxes[mine_back, :]

    for i in range(len(halos)):
        @pl.when(halos[i][4])
        def _():
            halo(i).wait_recv()

    tall = TILE + 2 * HALO
    row = lax.broadcasted_iota(jnp.int32, (tall, TILE), 0)
    lane = lax.broadcasted_iota(jnp.int32, (tall, TILE), 1)
    upright = jnp.where(
        row < HALO, gx, jnp.where(row < HALO + TILE, 1, m - 1 - gx)
    )
    sided_e = jnp.where(upright * (n - 1 - gy) > 0, got_e[...], 0.0)
    sided_w = jnp.where(upright * gy > 0, got_w[...], 0.0)
    for f in range(EVP):
        ext[f, HALO : 2 * HALO, :TILE] = jnp.where(has_up, got_t[f], 0.0)
        ext[f, 2 * HALO + TILE : 3 * HALO + TILE, :TILE] = jnp.where(has_down, got_b[f], 0.0)
        from_e = pltpu.roll(sided_e, TILE - HALO * f, 1) if f else sided_e
        from_w = pltpu.roll(sided_w, TILE - HALO * (f + 1), 1)
        ext[f, HALO : HALO + tall, TILE:] = jnp.where(
            lane < HALO, from_e, jnp.where(lane >= TILE - HALO, from_w, 0.0)
        )

    evp_steps(ext)
    for f in range(2):
        vel[f] = ext[f, inner, :TILE]
    for f in range(3):
        stress[f] = ext[2 + f, inner, :TILE]
    stores[1].start()
    stores[2].start()

    for k in reach:
        earriving(lax.rem(gy + k, n)).wait_recv()
    stores[3].start()
    for k in reach:
        farriving(lax.rem(gy + k, n)).wait_recv()
    stores[4].start()
    for g in range(groups):
        new_store(g).wait()
    for i in range(len(halos)):
        @pl.when(halos[i][3])
        def _():
            halo(i).wait_send()
    for k in reach:
        o = lax.rem(gy + k, n)
        sending(o).wait_send()
        esending(o).wait_send()
        fsending(o).wait_send()
    for copy in stores:
        copy.wait()


def column_step(g, j, slots, held, share, thick, drift, fluxes):
    at = pl.ds(pl.multiple_of(8 * g, 8), 8)
    cells = pl.ds(pl.multiple_of(TILE * j, TILE), TILE)
    ocean, salt, air, source, snowfall, wind = [
        slots[pl.ds(g * (64 * SENT) + 8 * f + j, 8, stride=8 * SENT), :] for f in range(SENT)
    ]
    filled = salt > 0.25
    air_resist = rcp(1.0 + 2.0 * wind)
    sums = None
    for c in range(CLASSES):
        area, floe, lying = share[c, at, cells], thick[c, at, cells], drift[c, at, cells]
        snow = lying + 0.3 * snowfall
        depth = floe * (1.0 / ICE)
        twice = 2.0 * depth
        snow_mass = snow * (2.0 / 3.0)
        snow_resist = snow * (1.0 / 0.9)
        snow_cond = rcp(snow_resist)
        top = rcp(0.5 * snow_resist + air_resist)
        above, resist = top, snow_resist
        ratios, values = [], []
        content = None
        for l in range(LAYERS):
            old = held[c, l, at, cells]
            if l < SNOW:
                mass = snow_mass
            else:
                brine = salt * (0.2 + 0.1 * (l - SNOW))
                mass = twice + twice * (0.2 * brine) * rcp(old * old + 0.1)
            if l < SNOW - 1:
                below = snow_cond
            elif l < LAYERS - 1:
                brine = salt * (0.2 + 0.1 * (l + 1 - SNOW))
                shifted = held[c, l + 1, at, cells] - 0.5
                later = depth * shifted * rcp(2.0 * shifted + 0.1 * brine)
                below = 2.0 * rcp(resist + later)
                resist = later
            else:
                below = 2.0 * rcp(resist)
            held_heat = mass * old
            content = held_heat if content is None else content + held_heat
            carried = held_heat
            pivot = mass + above + below
            if l == 0:
                carried = carried + top * air + source
            if l == LAYERS - 1:
                carried = carried + below * ocean
            if l > 0:
                pivot = pivot - above * ratios[-1]
                carried = carried + above * values[-1]
            inverse = rcp(pivot)
            ratios.append(below * inverse)
            values.append(carried * inverse)
            above = below
        new = values[-1]
        last = new
        held[c, LAYERS - 1, at, cells] = jnp.where(filled, new, held[c, LAYERS - 1, at, cells])
        for l in range(LAYERS - 2, -1, -1):
            new = values[l] + ratios[l] * new
            held[c, l, at, cells] = jnp.where(filled, new, held[c, l, at, cells])
        bottom_flux = below * (last - ocean)
        top_flux = top * (air - new)
        terms = [
            bottom_flux, top_flux, new, snow,
            0.05 * (content + top_flux - bottom_flux + source),
        ]
        terms = [area * term for term in terms]
        sums = terms if sums is None else [a + b for a, b in zip(sums, terms)]
    for f in range(BACK):
        fluxes[pl.ds(g * (64 * BACK) + 8 * f + j, 8, stride=8 * BACK), :] = sums[f]


def output_kernel(
    n, new_far, got_far, early_far, coef_far, vel_from, stress_from, holder, marker,
    warmth_far, out_far, vel_far, stress_far,
    held, got, got_early, coef, vel, stress, out, load_sem, store_sem,
):
    ways = [(got_far, got, None), (early_far, got_early, None), (coef_far, coef, None)]
    for c in range(CLASSES):
        ways.append((new_far.at[c], held.at[c], warmth_far.at[c]))
    ways += [(vel_from, vel, vel_far), (stress_from, stress, stress_far)]
    loads = [pltpu.make_async_copy(a, b, load_sem.at[i]) for i, (a, b, _) in enumerate(ways)]
    stores = [
        pltpu.make_async_copy(b, c, store_sem.at[i]) if c is not None else None
        for i, (_, b, c) in enumerate(ways)
    ]
    for copy in loads:
        copy.start()
    for load, store in zip(loads[3:], stores[3:]):
        load.wait()
        store.start()
    for copy in loads[:3]:
        copy.wait()
    bands = []
    rows_back, rows_early = 8 * BACK, 8 * EARLY
    for bx in range(BPX):
        pieces = []
        for by in range(BPY):
            b = bx * BPY + by
            rank = jnp.int32(0)
            for e in range(b):
                rank = rank + jnp.where(holder[e] == holder[b], 1 - marker[e], 0)
            sea = (1 - marker[b]).astype(jnp.float32)
            s = holder[b] * CAP + jnp.minimum(rank, CAP - 1)
            one = [got[pl.ds(pl.multiple_of(s * rows_back + 8 * f, 8), 8), :] for f in range(BACK)]
            two = [
                got_early[pl.ds(pl.multiple_of(s * rows_early + 8 * f, 8), 8), :]
                for f in range(EARLY)
            ]
            pieces.append([x * sea for x in one + two])
        parts = [swap_groups([piece[f] for piece in pieces]) for f in range(BACK + EARLY)]
        for q in range(4):
            place = pl.ds(BS * bx + q, 8, stride=4)
            bottom_flux, top_flux, warm, snow, energy, dim, floe = [part[q] for part in parts]
            out[0, place, :] = bottom_flux
            out[1, place, :] = top_flux
            out[2, place, :] = coef[0, place, :] * dim
            out[3, place, :] = warm
            out[4, place, :] = snow
            out[5, place, :] = floe - 0.05 * bottom_flux
            out[6, place, :] = energy
            out[7, place, :] = coef[1, place, :] * bottom_flux
        rows = pl.ds(BS * bx, BS)
        bands.append(pltpu.make_async_copy(
            out.at[:, rows, :], out_far.at[:, rows, :], store_sem.at[len(ways) + bx]
        ))
        bands[-1].start()
    for copy in stores[3:] + bands:
        copy.wait()


def local(
    interface_conditions, level_warmth_profile, class_coverage_share, class_floe_depth,
    class_drift_depth, floe_drift_speed, internal_tension_tensor, external_drive,
    floe_weight, floe_pressure, holder_lookup, ground_tile_marker,
):
    n, m = lax.axis_size("gy"), lax.axis_size("gx")
    f32 = jnp.float32
    smem = pl.BlockSpec(memory_space=pltpu.SMEM)
    hbm = pl.BlockSpec(memory_space=pltpu.HBM)
    shape = jax.ShapeDtypeStruct
    dma = pltpu.SemaphoreType.DMA
    holder = holder_lookup.reshape(-1)
    warmth = jnp.transpose(level_warmth_profile, (1, 2, 0, 3))
    share, thick, drift = [
        jnp.transpose(x, (1, 0, 2))
        for x in (class_coverage_share, class_floe_depth, class_drift_depth)
    ]
    places = n * CAP
    like = lambda x: pltpu.VMEM(x.shape, f32)
    held, got, got_early, coef, velocity, stress = pl.pallas_call(
        functools.partial(main_kernel, n, m),
        out_shape=(
            shape(warmth.shape, f32),
            shape((places * BACK * 8, TILE), f32),
            shape((places * EARLY * 8, TILE), f32),
            shape((2, TILE, TILE), f32),
            shape(floe_drift_speed.shape, f32),
            shape(internal_tension_tensor.shape, f32),
        ),
        in_specs=[hbm] * 6 + [smem] * 2 + [hbm] * 4,
        out_specs=(hbm,) * 6,
        scratch_shapes=[
            like(warmth),
            pltpu.VMEM((places * BACK * 8, TILE), f32),
            pltpu.VMEM((places * EARLY * 8, TILE), f32),
            pltpu.VMEM((2, TILE, TILE), f32),
            pltpu.SMEM((3, n), jnp.int32),
            like(interface_conditions), like(floe_drift_speed), like(internal_tension_tensor),
            like(external_drive), like(floe_weight), like(floe_pressure),
            like(share), like(thick), like(drift),
            pltpu.VMEM((B, SENT * 8, TILE), f32),
            pltpu.VMEM((places * SENT * 8, TILE), f32),
            pltpu.VMEM((places * SENT * 8, TILE), f32),
            pltpu.VMEM((places * EARLY * 8, TILE), f32),
            pltpu.VMEM((places * BACK * 8, TILE), f32),
            pltpu.VMEM((EVP, ROWS, 2 * TILE), f32),
            pltpu.VMEM((TILE, TILE), f32),
            pltpu.VMEM((TILE, TILE), f32),
            pltpu.VMEM((EVP, HALO, TILE), f32),
            pltpu.VMEM((EVP, HALO, TILE), f32),
            pltpu.VMEM((TILE + 2 * HALO, TILE), f32),
            pltpu.VMEM((TILE + 2 * HALO, TILE), f32),
            pltpu.VMEM((EVP, HALO, TILE), f32),
            pltpu.VMEM((EVP, HALO, TILE), f32),
            dma((9,)), dma((places // 8,)), dma((places // 8,)), dma((5,)),
            dma((n,)), dma((n,)), dma((n,)), dma((n,)), dma((n,)), dma((n,)),
            dma((8,)), dma((8,)),
        ],
        compiler_params=pltpu.CompilerParams(
            collective_id=0, has_side_effects=True, vmem_limit_bytes=VMEM_LIMIT
        ),
    )(
        interface_conditions, floe_drift_speed, internal_tension_tensor, external_drive,
        floe_weight, floe_pressure, holder, ground_tile_marker, warmth, share, thick, drift,
    )
    warmth, exchanges, velocity, stress = pl.pallas_call(
        functools.partial(output_kernel, n),
        out_shape=tuple(
            shape(x.shape, f32) for x in (held, interface_conditions, velocity, stress)
        ),
        in_specs=[hbm] * 6 + [smem] * 2,
        out_specs=(hbm,) * 4,
        scratch_shapes=[
            like(held), like(got), like(got_early), like(coef), like(velocity), like(stress),
            like(interface_conditions), dma((CLASSES + 5,)), dma((CLASSES + 5 + BPX,)),
        ],
        compiler_params=pltpu.CompilerParams(vmem_limit_bytes=VMEM_LIMIT),
    )(held, got, got_early, coef, velocity, stress, holder, ground_tile_marker)
    return jnp.transpose(warmth, (2, 0, 1, 3)), exchanges, velocity, stress


def solution(mesh):
    tile = P(None, "gx", "gy")
    owner = ("gx", "gy")
    return jax.shard_map(
        local,
        mesh=mesh,
        in_specs=(
            tile, P(owner, None, None, None), P(owner, None, None), P(owner, None, None),
            P(owner, None, None), tile, tile, tile, P("gx", "gy"), P("gx", "gy"),
            P(owner, None), P(owner),
        ),
        out_specs=(P(owner, None, None, None), tile, tile, tile),
        check_vma=False,
    )
```

```python
import functools

import jax
import jax.numpy as jnp
from jax import lax
from jax.experimental import pallas as pl
from jax.experimental.pallas import tpu as pltpu
from jax.sharding import PartitionSpec as P

MESH = pl.DeviceIdType.MESH
BS = 32
BPX = 4
BPY = 4
CAP = 2
ICE = 7
SNOW = 3
LAYERS = 10
CLASSES = 5
SUB = 4
B = 16
TILE = 128
SENT = 6
BACK = 5
EARLY = 2
EVP = 10
HALO = 8
ROWS = TILE + 4 * HALO
VMEM_LIMIT = 62 * 1024 * 1024


def rcp(x):
    return pl.reciprocal(x, approx=True)


def swap_groups(x):
    group = lax.broadcasted_iota(jnp.int32, x[0].shape, 1) // BS
    even = (group % 2) == 0
    low = group < 2
    y = [None] * 4
    for a in (0, 2):
        y[a] = jnp.where(even, x[a], pltpu.roll(x[a + 1], BS, 1))
        y[a + 1] = jnp.where(even, pltpu.roll(x[a], TILE - BS, 1), x[a + 1])
    z = [None] * 4
    for a in (0, 1):
        z[a] = jnp.where(low, y[a], pltpu.roll(y[a + 2], 2 * BS, 1))
        z[a + 2] = jnp.where(low, pltpu.roll(y[a], 2 * BS, 1), y[a + 2])
    return z


def evp_steps(ext):
    bands = [2 * HALO * i + HALO for i in range((TILE + 2 * HALO) // (2 * HALO))]
    size = 2 * HALO
    third = 1.0 / 1.5

    def d_row(f, r):
        return 0.5 * (ext[f, r + 1 : r + 1 + size, :] - ext[f, r - 1 : r - 1 + size, :])

    def d_lane(x):
        width = x.shape[1]
        return 0.5 * (pltpu.roll(x, width - 1, 1) - pltpu.roll(x, 1, 1))

    def step(_, carry):
        for r in bands:
            here = slice(r, r + size)
            ux, uy = d_row(0, r), d_lane(ext[0, here, :])
            vx, vy = d_row(1, r), d_lane(ext[1, here, :])
            diverge, tension, shearing = ux + vy, ux - vy, uy + vx
            square = diverge * diverge + 0.25 * (tension * tension + shearing * shearing) + 0.04
            inverse = lax.rsqrt(square)
            push = ext[9, here, :]
            scaled = push * inverse
            ext[2, here, :] = third * ext[2, here, :] + (scaled * diverge - push)
            ext[3, here, :] = third * ext[3, here, :] + 0.25 * (scaled * tension)
            ext[4, here, :] = third * ext[4, here, :] + 0.125 * (scaled * shearing)
        for r in bands:
            here = slice(r, r + size)
            force_x = 0.5 * (d_row(2, r) + d_row(3, r)) + d_lane(ext[4, here, :])
            force_y = 0.5 * d_lane(ext[2, here, :] - ext[3, here, :]) + d_row(4, r)
            east, north = ext[0, here, :], ext[1, here, :]
            half, keep = ext[5, here, :], ext[6, here, :]
            ext[0, here, :] = keep * (east + 0.15 * north) + half * force_x + ext[7, here, :]
            ext[1, here, :] = keep * (north - 0.15 * east) + half * force_y + ext[8, here, :]
        return carry

    lax.fori_loop(0, SUB, step, 0)


def parcels(n, gx, gy, rows, src, dst, send_sem, recv_sem):
    def sending(o):
        return pltpu.make_async_remote_copy(
            src_ref=src.at[pl.ds(o * rows, rows)], dst_ref=dst.at[pl.ds(gy * rows, rows)],
            send_sem=send_sem.at[o], recv_sem=recv_sem.at[gy],
            device_id=(gx, o), device_id_type=MESH,
        )

    def arriving(t):
        return pltpu.make_async_remote_copy(
            src_ref=src.at[pl.ds(t * rows, rows)], dst_ref=dst.at[pl.ds(t * rows, rows)],
            send_sem=send_sem.at[t], recv_sem=recv_sem.at[t],
            device_id=(gx, t), device_id_type=MESH,
        )

    return sending, arriving


def main_kernel(
    n, m,
    cond_far, vel_far, stress_far, drive_far, weight_far, pressure_far, holder, marker,
    warmth_far, share_far, thick_far, drift_far,
    new_far, got_far, early_far, coef_far, vel_out, stress_out,
    held, got, got_early, coef, picks, cond, vel, stress, drive, weight, pressure, share, thick, drift,
    blk, send, slots, early, fluxes,
    ext, pack_w, pack_e, top, bottom, got_w, got_e, got_t, got_b,
    in_sem, warm_sem, new_sem, out_sem, send_sem, recv_sem, esend_sem, erecv_sem, fsend_sem, frecv_sem,
    hsend_sem, hrecv_sem,
):
    gx, gy = lax.axis_index("gx"), lax.axis_index("gy")
    up, down = lax.rem(gx + m - 1, m), lax.rem(gx + 1, m)
    left, right = lax.rem(gy + n - 1, n), lax.rem(gy + 1, n)
    around = [(up, gy), (down, gy), (up, left), (up, right), (down, left), (down, right)]
    groups = n * CAP // 8
    per_group = 8 // CAP
    reach = sorted(range(1, n), key=lambda k: abs(k - n // 2))

    pairs = (
        (cond_far, cond), (share_far, share), (thick_far, thick), (drift_far, drift),
        (vel_far, vel), (stress_far, stress), (drive_far, drive),
        (weight_far, weight), (pressure_far, pressure),
    )
    loads = [pltpu.make_async_copy(a, b, in_sem.at[i]) for i, (a, b) in enumerate(pairs)]

    def warm_load(g):
        at = pl.ds(pl.multiple_of(8 * g, 8), 8)
        return pltpu.make_async_copy(
            warmth_far.at[:, :, at, :], held.at[:, :, at, :], warm_sem.at[g]
        )

    def new_store(g):
        at = pl.ds(pl.multiple_of(8 * g, 8), 8)
        return pltpu.make_async_copy(
            held.at[:, :, at, :], new_far.at[:, :, at, :], new_sem.at[g]
        )

    loads[0].start()
    barrier = pltpu.get_barrier_semaphore()
    for k in reach:
        pl.semaphore_signal(
            barrier, inc=1, device_id=(gx, lax.rem(gy + k, n)), device_id_type=MESH
        )
    for device in around:
        pl.semaphore_signal(barrier, inc=1, device_id=device, device_id_type=MESH)
    for copy in loads[1:]:
        copy.start()
    for g in range(groups):
        warm_load(g).start()

    def find(o, carry):
        count = jnp.int32(0)
        first = jnp.int32(0)
        second = jnp.int32(0)
        for b in range(B):
            hit = jnp.where(holder[b] == o, 1 - marker[b], 0)
            first = first + jnp.where(count == 0, hit * b, 0)
            second = second + jnp.where(count == 1, hit * b, 0)
            count = count + hit
        picks[0, o] = first
        picks[1, o] = second
        picks[2, o] = count
        return carry

    lax.fori_loop(0, n, find, 0)
    loads[0].wait()
    for bx in range(BPX):
        def part(f, q):
            return cond[f, pl.ds(BS * bx + q, 8, stride=4), :]

        for at, f in enumerate((0, 1, 2, None, 6, 7)):
            if f is None:
                pieces = [
                    0.25 * part(3, q) + 0.45 * part(4, q) + 0.3 * part(5, q) for q in range(4)
                ]
            else:
                pieces = [part(f, q) for q in range(4)]
            for by, piece in enumerate(swap_groups(pieces)):
                blk[bx * BPY + by, 8 * at : 8 * at + 8, :] = piece

    block_rows = SENT * 8

    def fill(o, carry):
        first, second, count = picks[0, o], picks[1, o], picks[2, o]
        has_first = jnp.where(count > 0, 1.0, 0.0)
        has_second = jnp.where(count > 1, 1.0, 0.0)
        at = pl.multiple_of(o * (CAP * block_rows), 8)
        send[pl.ds(at, block_rows), :] = blk[first] * has_first
        send[pl.ds(pl.multiple_of(at + block_rows, 8), block_rows), :] = blk[second] * has_second
        return carry

    pl.semaphore_wait(barrier, n - 1 + len(around))

    sending, arriving = parcels(
        n, gx, gy, CAP * block_rows, send, slots, send_sem, recv_sem
    )
    for k in reach:
        o = lax.rem(gy + k, n)
        fill(o, 0)
        sending(o).start()
    fill(gy, 0)
    mine = pl.ds(pl.multiple_of(gy * (CAP * block_rows), 8), CAP * block_rows)
    slots[mine, :] = send[mine, :]

    for copy in loads[1:4]:
        copy.wait()

    def ahead(i, carry):
        g, j = i // 8, lax.rem(i, 8)
        at = pl.ds(pl.multiple_of(8 * g, 8), 8)
        cells = pl.ds(pl.multiple_of(TILE * j, TILE), TILE)
        dim = jnp.zeros((8, TILE), jnp.float32)
        floe = jnp.zeros((8, TILE), jnp.float32)
        for c in range(CLASSES):
            area, deep = share[c, at, cells], thick[c, at, cells]
            dim = dim + area * jnp.exp(-5.0 * drift[c, at, cells] - 1.5 * deep)
            floe = floe + area * deep
        early[pl.ds(g * (8 * 16) + j, 8, stride=16), :] = dim
        early[pl.ds(g * (8 * 16) + 8 + j, 8, stride=16), :] = floe
        return carry

    lax.fori_loop(0, groups * 8, ahead, 0)
    esending, earriving = parcels(
        n, gx, gy, CAP * EARLY * 8, early, got_early, esend_sem, erecv_sem
    )
    mine_early = pl.ds(pl.multiple_of(gy * (CAP * EARLY * 8), 8), CAP * EARLY * 8)
    got_early[mine_early, :] = early[mine_early, :]

    for copy in loads[4:]:
        copy.wait()
    inner = slice(2 * HALO, 2 * HALO + TILE)
    ext[...] = jnp.zeros_like(ext)
    for f in range(2):
        ext[f, inner, :TILE] = vel[f]
    for f in range(3):
        ext[2 + f, inner, :TILE] = stress[f]
    column = lax.broadcasted_iota(jnp.int32, (BS, TILE), 1) // BS
    for bx in range(BPX):
        rows = slice(BS * bx, BS * bx + BS)
        into = slice(2 * HALO + BS * bx, 2 * HALO + BS * bx + BS)
        water = jnp.zeros((BS, TILE), jnp.float32)
        for by in range(BPY):
            sea = (1 - marker[bx * BPY + by]).astype(jnp.float32)
            water = jnp.where(column == by, sea, water)
        w = weight[rows, :]
        open_part = water * rcp(w + 0.5)
        half = 0.5 * open_part
        ext[5, into, :TILE] = half
        ext[6, into, :TILE] = open_part * w
        ext[7, into, :TILE] = half * (drive[0, rows, :] + drive[2, rows, :])
        ext[8, into, :TILE] = half * (drive[1, rows, :] + drive[3, rows, :])
        ext[9, into, :TILE] = pressure[rows, :] * (1.0 / 3.0)

    lane = lax.broadcasted_iota(jnp.int32, (TILE, TILE), 1)
    packed_w = jnp.zeros((TILE, TILE), jnp.float32)
    packed_e = jnp.zeros((TILE, TILE), jnp.float32)
    for f in range(EVP):
        own = (lane // HALO) == f
        x = ext[f, inner, :TILE]
        packed_w = jnp.where(own, pltpu.roll(x, HALO * f, 1) if f else x, packed_w)
        packed_e = jnp.where(own, pltpu.roll(x, HALO * (f + 1), 1), packed_e)
        top[f] = ext[f, 2 * HALO : 3 * HALO, :TILE]
        bottom[f] = ext[f, HALO + TILE : 2 * HALO + TILE, :TILE]
    pack_w[...] = packed_w
    pack_e[...] = packed_e

    head, tail = pl.ds(0, HALO), pl.ds(TILE - HALO, HALO)
    first, middle, last = pl.ds(0, HALO), pl.ds(HALO, TILE), pl.ds(HALO + TILE, HALO)
    has_up, has_down, has_left, has_right = gx > 0, gx < m - 1, gy > 0, gy < n - 1
    both = jnp.logical_and
    halos = [
        (pack_w, got_e.at[middle], (gx, left), has_left, has_right),
        (pack_e, got_w.at[middle], (gx, right), has_right, has_left),
        (top, got_b, (up, gy), has_up, has_down),
        (bottom, got_t, (down, gy), has_down, has_up),
        (pack_w.at[head], got_e.at[last], (up, left), both(has_up, has_left),
         both(has_down, has_right)),
        (pack_e.at[head], got_w.at[last], (up, right), both(has_up, has_right),
         both(has_down, has_left)),
        (pack_w.at[tail], got_e.at[first], (down, left), both(has_down, has_left),
         both(has_up, has_right)),
        (pack_e.at[tail], got_w.at[first], (down, right), both(has_down, has_right),
         both(has_up, has_left)),
    ]

    def halo(i):
        src, dst, device = halos[i][:3]
        return pltpu.make_async_remote_copy(
            src_ref=src, dst_ref=dst, send_sem=hsend_sem.at[i], recv_sem=hrecv_sem.at[i],
            device_id=device, device_id_type=MESH,
        )

    for i in range(len(halos)):
        @pl.when(halos[i][3])
        def _():
            halo(i).start()
    coef[0] = 0.7 * cond[3] * jnp.exp(-1.5 * cond[6])
    coef[1] = -0.05 * cond[1]
    results = ((coef, coef_far), (vel, vel_out), (stress, stress_out), (got_early, early_far), (got, got_far))
    stores = [pltpu.make_async_copy(a, b, out_sem.at[i]) for i, (a, b) in enumerate(results)]
    stores[0].start()

    fsending, farriving = parcels(n, gx, gy, CAP * BACK * 8, fluxes, got, fsend_sem, frecv_sem)
    own_group = gy // per_group
    for i in range(groups):
        g = lax.rem(own_group + i, groups)
        for e in range(per_group):
            t = g * per_group + e

            @pl.when(t != gy)
            def _():
                arriving(t).wait_recv()

        if i == min(1, groups - 1):
            for k in reach:
                esending(lax.rem(gy + k, n)).start()
        warm_load(g).wait()

        def chunk(j, carry):
            column_step(g, j, slots, held, share, thick, drift, fluxes)
            return carry

        lax.fori_loop(0, 8, chunk, 0)
        new_store(g).start()
        for e in range(per_group):
            t = g * per_group + e

            @pl.when(t != gy)
            def _():
                fsending(t).start()

    mine_back = pl.ds(pl.multiple_of(gy * (CAP * BACK * 8), 8), CAP * BACK * 8)
    got[mine_back, :] = fluxes[mine_back, :]

    for i in range(len(halos)):
        @pl.when(halos[i][4])
        def _():
            halo(i).wait_recv()

    tall = TILE + 2 * HALO
    row = lax.broadcasted_iota(jnp.int32, (tall, TILE), 0)
    lane = lax.broadcasted_iota(jnp.int32, (tall, TILE), 1)
    upright = jnp.where(
        row < HALO, gx, jnp.where(row < HALO + TILE, 1, m - 1 - gx)
    )
    sided_e = jnp.where(upright * (n - 1 - gy) > 0, got_e[...], 0.0)
    sided_w = jnp.where(upright * gy > 0, got_w[...], 0.0)
    for f in range(EVP):
        ext[f, HALO : 2 * HALO, :TILE] = jnp.where(has_up, got_t[f], 0.0)
        ext[f, 2 * HALO + TILE : 3 * HALO + TILE, :TILE] = jnp.where(has_down, got_b[f], 0.0)
        from_e = pltpu.roll(sided_e, TILE - HALO * f, 1) if f else sided_e
        from_w = pltpu.roll(sided_w, TILE - HALO * (f + 1), 1)
        ext[f, HALO : HALO + tall, TILE:] = jnp.where(
            lane < HALO, from_e, jnp.where(lane >= TILE - HALO, from_w, 0.0)
        )

    evp_steps(ext)
    for f in range(2):
        vel[f] = ext[f, inner, :TILE]
    for f in range(3):
        stress[f] = ext[2 + f, inner, :TILE]
    stores[1].start()
    stores[2].start()

    for k in reach:
        earriving(lax.rem(gy + k, n)).wait_recv()
    stores[3].start()
    for k in reach:
        farriving(lax.rem(gy + k, n)).wait_recv()
    stores[4].start()
    for g in range(groups):
        new_store(g).wait()
    for i in range(len(halos)):
        @pl.when(halos[i][3])
        def _():
            halo(i).wait_send()
    for k in reach:
        o = lax.rem(gy + k, n)
        sending(o).wait_send()
        esending(o).wait_send()
        fsending(o).wait_send()
    for copy in stores:
        copy.wait()


def column_step(g, j, slots, held, share, thick, drift, fluxes):
    at = pl.ds(pl.multiple_of(8 * g, 8), 8)
    cells = pl.ds(pl.multiple_of(TILE * j, TILE), TILE)
    ocean, salt, air, source, snowfall, wind = [
        slots[pl.ds(g * (64 * SENT) + 8 * f + j, 8, stride=8 * SENT), :] for f in range(SENT)
    ]
    filled = salt > 0.25
    air_resist = rcp(1.0 + 2.0 * wind)
    sums = None
    for c in range(CLASSES):
        area, floe, lying = share[c, at, cells], thick[c, at, cells], drift[c, at, cells]
        snow = lying + 0.3 * snowfall
        depth = floe * (1.0 / ICE)
        twice = 2.0 * depth
        snow_mass = snow * (2.0 / 3.0)
        snow_resist = snow * (1.0 / 0.9)
        snow_cond = rcp(snow_resist)
        top = rcp(0.5 * snow_resist + air_resist)
        above, resist = top, snow_resist
        ratios, values = [], []
        content = None
        for l in range(LAYERS):
            old = held[c, l, at, cells]
            if l < SNOW:
                mass = snow_mass
            else:
                brine = salt * (0.2 + 0.1 * (l - SNOW))
                mass = twice + twice * (0.2 * brine) * rcp(old * old + 0.1)
            if l < SNOW - 1:
                below = snow_cond
            elif l < LAYERS - 1:
                brine = salt * (0.2 + 0.1 * (l + 1 - SNOW))
                shifted = held[c, l + 1, at, cells] - 0.5
                later = depth * shifted * rcp(2.0 * shifted + 0.1 * brine)
                below = 2.0 * rcp(resist + later)
                resist = later
            else:
                below = 2.0 * rcp(resist)
            held_heat = mass * old
            content = held_heat if content is None else content + held_heat
            carried = held_heat
            pivot = mass + above + below
            if l == 0:
                carried = carried + top * air + source
            if l == LAYERS - 1:
                carried = carried + below * ocean
            if l > 0:
                pivot = pivot - above * ratios[-1]
                carried = carried + above * values[-1]
            inverse = rcp(pivot)
            ratios.append(below * inverse)
            values.append(carried * inverse)
            above = below
        new = values[-1]
        last = new
        held[c, LAYERS - 1, at, cells] = jnp.where(filled, new, held[c, LAYERS - 1, at, cells])
        for l in range(LAYERS - 2, -1, -1):
            new = values[l] + ratios[l] * new
            held[c, l, at, cells] = jnp.where(filled, new, held[c, l, at, cells])
        bottom_flux = below * (last - ocean)
        top_flux = top * (air - new)
        terms = [
            bottom_flux, top_flux, new, snow,
            0.05 * (content + top_flux - bottom_flux + source),
        ]
        terms = [area * term for term in terms]
        sums = terms if sums is None else [a + b for a, b in zip(sums, terms)]
    for f in range(BACK):
        fluxes[pl.ds(g * (64 * BACK) + 8 * f + j, 8, stride=8 * BACK), :] = sums[f]


def output_kernel(
    n, new_far, got_far, early_far, coef_far, vel_from, stress_from, holder, marker,
    warmth_far, out_far, vel_far, stress_far,
    held, got, got_early, coef, vel, stress, out, load_sem, store_sem,
):
    ways = [(got_far, got, None), (early_far, got_early, None), (coef_far, coef, None)]
    for c in range(CLASSES):
        ways.append((new_far.at[c], held.at[c], warmth_far.at[c]))
    ways += [(vel_from, vel, vel_far), (stress_from, stress, stress_far)]
    loads = [pltpu.make_async_copy(a, b, load_sem.at[i]) for i, (a, b, _) in enumerate(ways)]
    stores = [
        pltpu.make_async_copy(b, c, store_sem.at[i]) if c is not None else None
        for i, (_, b, c) in enumerate(ways)
    ]
    for copy in loads:
        copy.start()
    bands = []
    spots = []
    for b in range(B):
        rank = jnp.int32(0)
        for e in range(b):
            rank = rank + jnp.where(holder[e] == holder[b], 1 - marker[e], 0)
        spots.append(holder[b] * CAP + jnp.minimum(rank, CAP - 1))
    for copy in loads[:3]:
        copy.wait()
    rows_back, rows_early = 8 * BACK, 8 * EARLY
    for bx in range(BPX):
        pieces = []
        for by in range(BPY):
            b = bx * BPY + by
            sea = (1 - marker[b]).astype(jnp.float32)
            s = spots[b]
            one = [got[pl.ds(pl.multiple_of(s * rows_back + 8 * f, 8), 8), :] for f in range(BACK)]
            two = [
                got_early[pl.ds(pl.multiple_of(s * rows_early + 8 * f, 8), 8), :]
                for f in range(EARLY)
            ]
            pieces.append([x * sea for x in one + two])
        parts = [swap_groups([piece[f] for piece in pieces]) for f in range(BACK + EARLY)]
        for q in range(4):
            place = pl.ds(BS * bx + q, 8, stride=4)
            bottom_flux, top_flux, warm, snow, energy, dim, floe = [part[q] for part in parts]
            out[0, place, :] = bottom_flux
            out[1, place, :] = top_flux
            out[2, place, :] = coef[0, place, :] * dim
            out[3, place, :] = warm
            out[4, place, :] = snow
            out[5, place, :] = floe - 0.05 * bottom_flux
            out[6, place, :] = energy
            out[7, place, :] = coef[1, place, :] * bottom_flux
        rows = pl.ds(BS * bx, BS)
        bands.append(pltpu.make_async_copy(
            out.at[:, rows, :], out_far.at[:, rows, :], store_sem.at[len(ways) + bx]
        ))
        bands[-1].start()
        for at in range(3 + bx, len(ways), BPX):
            loads[at].wait()
            stores[at].start()
    for copy in stores[3:] + bands:
        copy.wait()


def local(
    interface_conditions, level_warmth_profile, class_coverage_share, class_floe_depth,
    class_drift_depth, floe_drift_speed, internal_tension_tensor, external_drive,
    floe_weight, floe_pressure, holder_lookup, ground_tile_marker,
):
    n, m = lax.axis_size("gy"), lax.axis_size("gx")
    f32 = jnp.float32
    smem = pl.BlockSpec(memory_space=pltpu.SMEM)
    hbm = pl.BlockSpec(memory_space=pltpu.HBM)
    shape = jax.ShapeDtypeStruct
    dma = pltpu.SemaphoreType.DMA
    holder = holder_lookup.reshape(-1)
    warmth = jnp.transpose(level_warmth_profile, (1, 2, 0, 3))
    share, thick, drift = [
        jnp.transpose(x, (1, 0, 2))
        for x in (class_coverage_share, class_floe_depth, class_drift_depth)
    ]
    places = n * CAP
    like = lambda x: pltpu.VMEM(x.shape, f32)
    held, got, got_early, coef, velocity, stress = pl.pallas_call(
        functools.partial(main_kernel, n, m),
        out_shape=(
            shape(warmth.shape, f32),
            shape((places * BACK * 8, TILE), f32),
            shape((places * EARLY * 8, TILE), f32),
            shape((2, TILE, TILE), f32),
            shape(floe_drift_speed.shape, f32),
            shape(internal_tension_tensor.shape, f32),
        ),
        in_specs=[hbm] * 6 + [smem] * 2 + [hbm] * 4,
        out_specs=(hbm,) * 6,
        scratch_shapes=[
            like(warmth),
            pltpu.VMEM((places * BACK * 8, TILE), f32),
            pltpu.VMEM((places * EARLY * 8, TILE), f32),
            pltpu.VMEM((2, TILE, TILE), f32),
            pltpu.SMEM((3, n), jnp.int32),
            like(interface_conditions), like(floe_drift_speed), like(internal_tension_tensor),
            like(external_drive), like(floe_weight), like(floe_pressure),
            like(share), like(thick), like(drift),
            pltpu.VMEM((B, SENT * 8, TILE), f32),
            pltpu.VMEM((places * SENT * 8, TILE), f32),
            pltpu.VMEM((places * SENT * 8, TILE), f32),
            pltpu.VMEM((places * EARLY * 8, TILE), f32),
            pltpu.VMEM((places * BACK * 8, TILE), f32),
            pltpu.VMEM((EVP, ROWS, 2 * TILE), f32),
            pltpu.VMEM((TILE, TILE), f32),
            pltpu.VMEM((TILE, TILE), f32),
            pltpu.VMEM((EVP, HALO, TILE), f32),
            pltpu.VMEM((EVP, HALO, TILE), f32),
            pltpu.VMEM((TILE + 2 * HALO, TILE), f32),
            pltpu.VMEM((TILE + 2 * HALO, TILE), f32),
            pltpu.VMEM((EVP, HALO, TILE), f32),
            pltpu.VMEM((EVP, HALO, TILE), f32),
            dma((9,)), dma((places // 8,)), dma((places // 8,)), dma((5,)),
            dma((n,)), dma((n,)), dma((n,)), dma((n,)), dma((n,)), dma((n,)),
            dma((8,)), dma((8,)),
        ],
        compiler_params=pltpu.CompilerParams(
            collective_id=0, has_side_effects=True, vmem_limit_bytes=VMEM_LIMIT
        ),
    )(
        interface_conditions, floe_drift_speed, internal_tension_tensor, external_drive,
        floe_weight, floe_pressure, holder, ground_tile_marker, warmth, share, thick, drift,
    )
    warmth, exchanges, velocity, stress = pl.pallas_call(
        functools.partial(output_kernel, n),
        out_shape=tuple(
            shape(x.shape, f32) for x in (held, interface_conditions, velocity, stress)
        ),
        in_specs=[hbm] * 6 + [smem] * 2,
        out_specs=(hbm,) * 4,
        scratch_shapes=[
            like(held), like(got), like(got_early), like(coef), like(velocity), like(stress),
            like(interface_conditions), dma((CLASSES + 5,)), dma((CLASSES + 5 + BPX,)),
        ],
        compiler_params=pltpu.CompilerParams(vmem_limit_bytes=VMEM_LIMIT),
    )(held, got, got_early, coef, velocity, stress, holder, ground_tile_marker)
    return jnp.transpose(warmth, (2, 0, 1, 3)), exchanges, velocity, stress


def solution(mesh):
    tile = P(None, "gx", "gy")
    owner = ("gx", "gy")
    return jax.shard_map(
        local,
        mesh=mesh,
        in_specs=(
            tile, P(owner, None, None, None), P(owner, None, None), P(owner, None, None),
            P(owner, None, None), tile, tile, tile, P("gx", "gy"), P("gx", "gy"),
            P(owner, None), P(owner),
        ),
        out_specs=(P(owner, None, None, None), tile, tile, tile),
        check_vma=False,
    )
```

```python
import functools

import jax
import jax.numpy as jnp
from jax import lax
from jax.experimental import pallas as pl
from jax.experimental.pallas import tpu as pltpu
from jax.sharding import PartitionSpec as P

MESH = pl.DeviceIdType.MESH
BS = 32
BPX = 4
BPY = 4
CAP = 2
ICE = 7
SNOW = 3
LAYERS = 10
CLASSES = 5
SUB = 4
B = 16
TILE = 128
SENT = 6
BACK = 5
EARLY = 2
EVP = 10
HALO = 8
ROWS = TILE + 4 * HALO
VMEM_LIMIT = 62 * 1024 * 1024


def rcp(x):
    return pl.reciprocal(x, approx=True)


def swap_groups(x):
    group = lax.broadcasted_iota(jnp.int32, x[0].shape, 1) // BS
    even = (group % 2) == 0
    low = group < 2
    y = [None] * 4
    for a in (0, 2):
        y[a] = jnp.where(even, x[a], pltpu.roll(x[a + 1], BS, 1))
        y[a + 1] = jnp.where(even, pltpu.roll(x[a], TILE - BS, 1), x[a + 1])
    z = [None] * 4
    for a in (0, 1):
        z[a] = jnp.where(low, y[a], pltpu.roll(y[a + 2], 2 * BS, 1))
        z[a + 2] = jnp.where(low, pltpu.roll(y[a], 2 * BS, 1), y[a + 2])
    return z


def evp_steps(ext):
    bands = [2 * HALO * i + HALO for i in range((TILE + 2 * HALO) // (2 * HALO))]
    size = 2 * HALO
    third = 1.0 / 1.5

    def d_row(f, r):
        return 0.5 * (ext[f, r + 1 : r + 1 + size, :] - ext[f, r - 1 : r - 1 + size, :])

    def d_lane(x):
        width = x.shape[1]
        return 0.5 * (pltpu.roll(x, width - 1, 1) - pltpu.roll(x, 1, 1))

    def step(_, carry):
        for r in bands:
            here = slice(r, r + size)
            ux, uy = d_row(0, r), d_lane(ext[0, here, :])
            vx, vy = d_row(1, r), d_lane(ext[1, here, :])
            diverge, tension, shearing = ux + vy, ux - vy, uy + vx
            square = diverge * diverge + 0.25 * (tension * tension + shearing * shearing) + 0.04
            inverse = lax.rsqrt(square)
            push = ext[9, here, :]
            scaled = push * inverse
            ext[2, here, :] = third * ext[2, here, :] + (scaled * diverge - push)
            ext[3, here, :] = third * ext[3, here, :] + 0.25 * (scaled * tension)
            ext[4, here, :] = third * ext[4, here, :] + 0.125 * (scaled * shearing)
        for r in bands:
            here = slice(r, r + size)
            force_x = 0.5 * (d_row(2, r) + d_row(3, r)) + d_lane(ext[4, here, :])
            force_y = 0.5 * d_lane(ext[2, here, :] - ext[3, here, :]) + d_row(4, r)
            east, north = ext[0, here, :], ext[1, here, :]
            half, keep = ext[5, here, :], ext[6, here, :]
            ext[0, here, :] = keep * (east + 0.15 * north) + half * force_x + ext[7, here, :]
            ext[1, here, :] = keep * (north - 0.15 * east) + half * force_y + ext[8, here, :]
        return carry

    lax.fori_loop(0, SUB, step, 0)


def parcels(n, gx, gy, rows, src, dst, send_sem, recv_sem):
    def sending(o):
        return pltpu.make_async_remote_copy(
            src_ref=src.at[pl.ds(o * rows, rows)], dst_ref=dst.at[pl.ds(gy * rows, rows)],
            send_sem=send_sem.at[o], recv_sem=recv_sem.at[gy],
            device_id=(gx, o), device_id_type=MESH,
        )

    def arriving(t):
        return pltpu.make_async_remote_copy(
            src_ref=src.at[pl.ds(t * rows, rows)], dst_ref=dst.at[pl.ds(t * rows, rows)],
            send_sem=send_sem.at[t], recv_sem=recv_sem.at[t],
            device_id=(gx, t), device_id_type=MESH,
        )

    return sending, arriving


def main_kernel(
    n, m,
    cond_far, vel_far, stress_far, drive_far, weight_far, pressure_far, holder, marker,
    warmth_far, share_far, thick_far, drift_far,
    new_far, got_far, early_far, coef_far, vel_out, stress_out,
    held, got, got_early, coef, picks, cond, vel, stress, drive, weight, pressure, share, thick, drift,
    blk, send, slots, early, fluxes,
    ext, pack_w, pack_e, top, bottom, got_w, got_e, got_t, got_b,
    in_sem, band_sem, warm_sem, new_sem, out_sem, got_sem, send_sem, recv_sem, esend_sem, erecv_sem, fsend_sem, frecv_sem,
    hsend_sem, hrecv_sem,
):
    gx, gy = lax.axis_index("gx"), lax.axis_index("gy")
    up, down = lax.rem(gx + m - 1, m), lax.rem(gx + 1, m)
    left, right = lax.rem(gy + n - 1, n), lax.rem(gy + 1, n)
    around = [(up, gy), (down, gy), (up, left), (up, right), (down, left), (down, right)]
    groups = n * CAP // 8
    per_group = 8 // CAP
    reach = sorted(range(1, n), key=lambda k: abs(k - n // 2))

    pairs = (
        (share_far, share), (thick_far, thick), (drift_far, drift),
        (vel_far, vel), (stress_far, stress), (drive_far, drive),
        (weight_far, weight), (pressure_far, pressure),
    )
    loads = [pltpu.make_async_copy(a, b, in_sem.at[i]) for i, (a, b) in enumerate(pairs)]

    def warm_load(g):
        at = pl.ds(pl.multiple_of(8 * g, 8), 8)
        return pltpu.make_async_copy(
            warmth_far.at[:, :, at, :], held.at[:, :, at, :], warm_sem.at[g]
        )

    def new_store(g):
        at = pl.ds(pl.multiple_of(8 * g, 8), 8)
        return pltpu.make_async_copy(
            held.at[:, :, at, :], new_far.at[:, :, at, :], new_sem.at[g]
        )

    field_loads = []
    for bx in range(BPX):
        rows = pl.ds(BS * bx, BS)
        field_loads.append(pltpu.make_async_copy(
            cond_far.at[:, rows, :], cond.at[:, rows, :], band_sem.at[bx]
        ))
        field_loads[-1].start()
    barrier = pltpu.get_barrier_semaphore()
    for k in reach:
        pl.semaphore_signal(
            barrier, inc=1, device_id=(gx, lax.rem(gy + k, n)), device_id_type=MESH
        )
    for device in around:
        pl.semaphore_signal(barrier, inc=1, device_id=device, device_id_type=MESH)
    for copy in loads:
        copy.start()
    for g in range(groups):
        warm_load(g).start()

    def find(o, carry):
        count = jnp.int32(0)
        first = jnp.int32(0)
        second = jnp.int32(0)
        for b in range(B):
            hit = jnp.where(holder[b] == o, 1 - marker[b], 0)
            first = first + jnp.where(count == 0, hit * b, 0)
            second = second + jnp.where(count == 1, hit * b, 0)
            count = count + hit
        picks[0, o] = first
        picks[1, o] = second
        picks[2, o] = count
        return carry

    lax.fori_loop(0, n, find, 0)
    for bx in range(BPX):
        field_loads[bx].wait()

        def part(f, q):
            return cond[f, pl.ds(BS * bx + q, 8, stride=4), :]

        for at, f in enumerate((0, 1, 2, None, 6, 7)):
            if f is None:
                pieces = [
                    0.25 * part(3, q) + 0.45 * part(4, q) + 0.3 * part(5, q) for q in range(4)
                ]
            else:
                pieces = [part(f, q) for q in range(4)]
            for by, piece in enumerate(swap_groups(pieces)):
                blk[bx * BPY + by, 8 * at : 8 * at + 8, :] = piece

    block_rows = SENT * 8

    def fill(o, carry):
        first, second, count = picks[0, o], picks[1, o], picks[2, o]
        has_first = jnp.where(count > 0, 1.0, 0.0)
        has_second = jnp.where(count > 1, 1.0, 0.0)
        at = pl.multiple_of(o * (CAP * block_rows), 8)
        send[pl.ds(at, block_rows), :] = blk[first] * has_first
        send[pl.ds(pl.multiple_of(at + block_rows, 8), block_rows), :] = blk[second] * has_second
        return carry

    pl.semaphore_wait(barrier, n - 1 + len(around))

    sending, arriving = parcels(
        n, gx, gy, CAP * block_rows, send, slots, send_sem, recv_sem
    )
    for k in reach:
        o = lax.rem(gy + k, n)
        fill(o, 0)
        sending(o).start()
    fill(gy, 0)
    mine = pl.ds(pl.multiple_of(gy * (CAP * block_rows), 8), CAP * block_rows)
    slots[mine, :] = send[mine, :]

    for copy in loads[:3]:
        copy.wait()

    def ahead(i, carry):
        g, j = i // 8, lax.rem(i, 8)
        at = pl.ds(pl.multiple_of(8 * g, 8), 8)
        cells = pl.ds(pl.multiple_of(TILE * j, TILE), TILE)
        dim = jnp.zeros((8, TILE), jnp.float32)
        floe = jnp.zeros((8, TILE), jnp.float32)
        for c in range(CLASSES):
            area, deep = share[c, at, cells], thick[c, at, cells]
            dim = dim + area * jnp.exp(-5.0 * drift[c, at, cells] - 1.5 * deep)
            floe = floe + area * deep
        early[pl.ds(g * (8 * 16) + j, 8, stride=16), :] = dim
        early[pl.ds(g * (8 * 16) + 8 + j, 8, stride=16), :] = floe
        return carry

    lax.fori_loop(0, groups * 8, ahead, 0)
    esending, earriving = parcels(
        n, gx, gy, CAP * EARLY * 8, early, got_early, esend_sem, erecv_sem
    )
    mine_early = pl.ds(pl.multiple_of(gy * (CAP * EARLY * 8), 8), CAP * EARLY * 8)
    got_early[mine_early, :] = early[mine_early, :]

    for copy in loads[3:]:
        copy.wait()
    inner = slice(2 * HALO, 2 * HALO + TILE)
    ext[...] = jnp.zeros_like(ext)
    for f in range(2):
        ext[f, inner, :TILE] = vel[f]
    for f in range(3):
        ext[2 + f, inner, :TILE] = stress[f]
    column = lax.broadcasted_iota(jnp.int32, (BS, TILE), 1) // BS
    for bx in range(BPX):
        rows = slice(BS * bx, BS * bx + BS)
        into = slice(2 * HALO + BS * bx, 2 * HALO + BS * bx + BS)
        water = jnp.zeros((BS, TILE), jnp.float32)
        for by in range(BPY):
            sea = (1 - marker[bx * BPY + by]).astype(jnp.float32)
            water = jnp.where(column == by, sea, water)
        w = weight[rows, :]
        open_part = water * rcp(w + 0.5)
        half = 0.5 * open_part
        ext[5, into, :TILE] = half
        ext[6, into, :TILE] = open_part * w
        ext[7, into, :TILE] = half * (drive[0, rows, :] + drive[2, rows, :])
        ext[8, into, :TILE] = half * (drive[1, rows, :] + drive[3, rows, :])
        ext[9, into, :TILE] = pressure[rows, :] * (1.0 / 3.0)

    lane = lax.broadcasted_iota(jnp.int32, (TILE, TILE), 1)
    packed_w = jnp.zeros((TILE, TILE), jnp.float32)
    packed_e = jnp.zeros((TILE, TILE), jnp.float32)
    for f in range(EVP):
        own = (lane // HALO) == f
        x = ext[f, inner, :TILE]
        packed_w = jnp.where(own, pltpu.roll(x, HALO * f, 1) if f else x, packed_w)
        packed_e = jnp.where(own, pltpu.roll(x, HALO * (f + 1), 1), packed_e)
        top[f] = ext[f, 2 * HALO : 3 * HALO, :TILE]
        bottom[f] = ext[f, HALO + TILE : 2 * HALO + TILE, :TILE]
    pack_w[...] = packed_w
    pack_e[...] = packed_e

    head, tail = pl.ds(0, HALO), pl.ds(TILE - HALO, HALO)
    first, middle, last = pl.ds(0, HALO), pl.ds(HALO, TILE), pl.ds(HALO + TILE, HALO)
    has_up, has_down, has_left, has_right = gx > 0, gx < m - 1, gy > 0, gy < n - 1
    both = jnp.logical_and
    halos = [
        (pack_w, got_e.at[middle], (gx, left), has_left, has_right),
        (pack_e, got_w.at[middle], (gx, right), has_right, has_left),
        (top, got_b, (up, gy), has_up, has_down),
        (bottom, got_t, (down, gy), has_down, has_up),
        (pack_w.at[head], got_e.at[last], (up, left), both(has_up, has_left),
         both(has_down, has_right)),
        (pack_e.at[head], got_w.at[last], (up, right), both(has_up, has_right),
         both(has_down, has_left)),
        (pack_w.at[tail], got_e.at[first], (down, left), both(has_down, has_left),
         both(has_up, has_right)),
        (pack_e.at[tail], got_w.at[first], (down, right), both(has_down, has_right),
         both(has_up, has_left)),
    ]

    def halo(i):
        src, dst, device = halos[i][:3]
        return pltpu.make_async_remote_copy(
            src_ref=src, dst_ref=dst, send_sem=hsend_sem.at[i], recv_sem=hrecv_sem.at[i],
            device_id=device, device_id_type=MESH,
        )

    for i in range(len(halos)):
        @pl.when(halos[i][3])
        def _():
            halo(i).start()
    coef[0] = 0.7 * cond[3] * jnp.exp(-1.5 * cond[6])
    coef[1] = -0.05 * cond[1]
    results = ((coef, coef_far), (vel, vel_out), (stress, stress_out), (got_early, early_far))
    stores = [pltpu.make_async_copy(a, b, out_sem.at[i]) for i, (a, b) in enumerate(results)]
    stores[0].start()

    fsending, farriving = parcels(n, gx, gy, CAP * BACK * 8, fluxes, got, fsend_sem, frecv_sem)
    own_group = gy // per_group
    for i in range(groups):
        g = lax.rem(own_group + i, groups)
        for e in range(per_group):
            t = g * per_group + e

            @pl.when(t != gy)
            def _():
                arriving(t).wait_recv()

        if i == min(1, groups - 1):
            for k in reach:
                esending(lax.rem(gy + k, n)).start()
        warm_load(g).wait()

        def chunk(j, carry):
            column_step(g, j, slots, held, share, thick, drift, fluxes)
            return carry

        lax.fori_loop(0, 8, chunk, 0)
        new_store(g).start()
        for e in range(per_group):
            t = g * per_group + e

            @pl.when(t != gy)
            def _():
                fsending(t).start()

    mine_back = pl.ds(pl.multiple_of(gy * (CAP * BACK * 8), 8), CAP * BACK * 8)
    got[mine_back, :] = fluxes[mine_back, :]

    for i in range(len(halos)):
        @pl.when(halos[i][4])
        def _():
            halo(i).wait_recv()

    tall = TILE + 2 * HALO
    row = lax.broadcasted_iota(jnp.int32, (tall, TILE), 0)
    lane = lax.broadcasted_iota(jnp.int32, (tall, TILE), 1)
    upright = jnp.where(
        row < HALO, gx, jnp.where(row < HALO + TILE, 1, m - 1 - gx)
    )
    sided_e = jnp.where(upright * (n - 1 - gy) > 0, got_e[...], 0.0)
    sided_w = jnp.where(upright * gy > 0, got_w[...], 0.0)
    for f in range(EVP):
        ext[f, HALO : 2 * HALO, :TILE] = jnp.where(has_up, got_t[f], 0.0)
        ext[f, 2 * HALO + TILE : 3 * HALO + TILE, :TILE] = jnp.where(has_down, got_b[f], 0.0)
        from_e = pltpu.roll(sided_e, TILE - HALO * f, 1) if f else sided_e
        from_w = pltpu.roll(sided_w, TILE - HALO * (f + 1), 1)
        ext[f, HALO : HALO + tall, TILE:] = jnp.where(
            lane < HALO, from_e, jnp.where(lane >= TILE - HALO, from_w, 0.0)
        )

    evp_steps(ext)
    for f in range(2):
        vel[f] = ext[f, inner, :TILE]
    for f in range(3):
        stress[f] = ext[2 + f, inner, :TILE]
    stores[1].start()
    stores[2].start()

    for k in reach:
        earriving(lax.rem(gy + k, n)).wait_recv()
    stores[3].start()
    back_rows = CAP * BACK * 8

    def got_store(t):
        at = pl.ds(pl.multiple_of(t * back_rows, 8), back_rows)
        return pltpu.make_async_copy(got.at[at], got_far.at[at], got_sem.at[t])

    got_store(gy).start()
    for k in reversed(reach):
        t = lax.rem(gy + k, n)
        farriving(t).wait_recv()
        got_store(t).start()
    for g in range(groups):
        new_store(g).wait()
    for i in range(len(halos)):
        @pl.when(halos[i][3])
        def _():
            halo(i).wait_send()
    for k in reach:
        o = lax.rem(gy + k, n)
        sending(o).wait_send()
        esending(o).wait_send()
        fsending(o).wait_send()
    for copy in stores:
        copy.wait()
    for t in range(n):
        got_store(t).wait()


def column_step(g, j, slots, held, share, thick, drift, fluxes):
    at = pl.ds(pl.multiple_of(8 * g, 8), 8)
    cells = pl.ds(pl.multiple_of(TILE * j, TILE), TILE)
    ocean, salt, air, source, snowfall, wind = [
        slots[pl.ds(g * (64 * SENT) + 8 * f + j, 8, stride=8 * SENT), :] for f in range(SENT)
    ]
    filled = salt > 0.25
    air_resist = rcp(1.0 + 2.0 * wind)
    sums = None
    for c in range(CLASSES):
        area, floe, lying = share[c, at, cells], thick[c, at, cells], drift[c, at, cells]
        snow = lying + 0.3 * snowfall
        depth = floe * (1.0 / ICE)
        twice = 2.0 * depth
        snow_mass = snow * (2.0 / 3.0)
        snow_resist = snow * (1.0 / 0.9)
        snow_cond = rcp(snow_resist)
        top = rcp(0.5 * snow_resist + air_resist)
        above, resist = top, snow_resist
        ratios, values = [], []
        content = None
        for l in range(LAYERS):
            old = held[c, l, at, cells]
            if l < SNOW:
                mass = snow_mass
            else:
                brine = salt * (0.2 + 0.1 * (l - SNOW))
                mass = twice + twice * (0.2 * brine) * rcp(old * old + 0.1)
            if l < SNOW - 1:
                below = snow_cond
            elif l < LAYERS - 1:
                brine = salt * (0.2 + 0.1 * (l + 1 - SNOW))
                shifted = held[c, l + 1, at, cells] - 0.5
                later = depth * shifted * rcp(2.0 * shifted + 0.1 * brine)
                below = 2.0 * rcp(resist + later)
                resist = later
            else:
                below = 2.0 * rcp(resist)
            held_heat = mass * old
            content = held_heat if content is None else content + held_heat
            carried = held_heat
            pivot = mass + above + below
            if l == 0:
                carried = carried + top * air + source
            if l == LAYERS - 1:
                carried = carried + below * ocean
            if l > 0:
                pivot = pivot - above * ratios[-1]
                carried = carried + above * values[-1]
            inverse = rcp(pivot)
            ratios.append(below * inverse)
            values.append(carried * inverse)
            above = below
        new = values[-1]
        last = new
        held[c, LAYERS - 1, at, cells] = jnp.where(filled, new, held[c, LAYERS - 1, at, cells])
        for l in range(LAYERS - 2, -1, -1):
            new = values[l] + ratios[l] * new
            held[c, l, at, cells] = jnp.where(filled, new, held[c, l, at, cells])
        bottom_flux = below * (last - ocean)
        top_flux = top * (air - new)
        terms = [
            bottom_flux, top_flux, new, snow,
            0.05 * (content + top_flux - bottom_flux + source),
        ]
        terms = [area * term for term in terms]
        sums = terms if sums is None else [a + b for a, b in zip(sums, terms)]
    for f in range(BACK):
        fluxes[pl.ds(g * (64 * BACK) + 8 * f + j, 8, stride=8 * BACK), :] = sums[f]


def output_kernel(
    n, new_far, got_far, early_far, coef_far, vel_from, stress_from, holder, marker,
    warmth_far, out_far, vel_far, stress_far,
    held, got, got_early, coef, vel, stress, out, load_sem, store_sem,
):
    ways = [(got_far, got, None), (early_far, got_early, None), (coef_far, coef, None)]
    for c in range(CLASSES):
        for h in range(2):
            half = pl.ds(h * (LAYERS // 2), LAYERS // 2)
            ways.append((new_far.at[c, half], held.at[c, half], warmth_far.at[c, half]))
    ways += [(vel_from, vel, vel_far), (stress_from, stress, stress_far)]
    loads = [pltpu.make_async_copy(a, b, load_sem.at[i]) for i, (a, b, _) in enumerate(ways)]
    stores = [
        pltpu.make_async_copy(b, c, store_sem.at[i]) if c is not None else None
        for i, (_, b, c) in enumerate(ways)
    ]
    for copy in loads:
        copy.start()
    bands = []
    spots = []
    for b in range(B):
        rank = jnp.int32(0)
        for e in range(b):
            rank = rank + jnp.where(holder[e] == holder[b], 1 - marker[e], 0)
        spots.append(holder[b] * CAP + jnp.minimum(rank, CAP - 1))
    for copy in loads[:3]:
        copy.wait()
    rows_back, rows_early = 8 * BACK, 8 * EARLY
    for bx in range(BPX):
        pieces = []
        for by in range(BPY):
            b = bx * BPY + by
            sea = (1 - marker[b]).astype(jnp.float32)
            s = spots[b]
            one = [got[pl.ds(pl.multiple_of(s * rows_back + 8 * f, 8), 8), :] for f in range(BACK)]
            two = [
                got_early[pl.ds(pl.multiple_of(s * rows_early + 8 * f, 8), 8), :]
                for f in range(EARLY)
            ]
            pieces.append([x * sea for x in one + two])
        parts = [swap_groups([piece[f] for piece in pieces]) for f in range(BACK + EARLY)]
        for q in range(4):
            place = pl.ds(BS * bx + q, 8, stride=4)
            bottom_flux, top_flux, warm, snow, energy, dim, floe = [part[q] for part in parts]
            out[0, place, :] = bottom_flux
            out[1, place, :] = top_flux
            out[2, place, :] = coef[0, place, :] * dim
            out[3, place, :] = warm
            out[4, place, :] = snow
            out[5, place, :] = floe - 0.05 * bottom_flux
            out[6, place, :] = energy
            out[7, place, :] = coef[1, place, :] * bottom_flux
        rows = pl.ds(BS * bx, BS)
        bands.append(pltpu.make_async_copy(
            out.at[:, rows, :], out_far.at[:, rows, :], store_sem.at[len(ways) + bx]
        ))
        bands[-1].start()
        for at in range(3 + bx, len(ways), BPX):
            loads[at].wait()
            stores[at].start()
    for copy in stores[3:] + bands:
        copy.wait()


def local(
    interface_conditions, level_warmth_profile, class_coverage_share, class_floe_depth,
    class_drift_depth, floe_drift_speed, internal_tension_tensor, external_drive,
    floe_weight, floe_pressure, holder_lookup, ground_tile_marker,
):
    n, m = lax.axis_size("gy"), lax.axis_size("gx")
    f32 = jnp.float32
    smem = pl.BlockSpec(memory_space=pltpu.SMEM)
    hbm = pl.BlockSpec(memory_space=pltpu.HBM)
    shape = jax.ShapeDtypeStruct
    dma = pltpu.SemaphoreType.DMA
    holder = holder_lookup.reshape(-1)
    warmth = jnp.transpose(level_warmth_profile, (1, 2, 0, 3))
    share, thick, drift = [
        jnp.transpose(x, (1, 0, 2))
        for x in (class_coverage_share, class_floe_depth, class_drift_depth)
    ]
    places = n * CAP
    like = lambda x: pltpu.VMEM(x.shape, f32)
    held, got, got_early, coef, velocity, stress = pl.pallas_call(
        functools.partial(main_kernel, n, m),
        out_shape=(
            shape(warmth.shape, f32),
            shape((places * BACK * 8, TILE), f32),
            shape((places * EARLY * 8, TILE), f32),
            shape((2, TILE, TILE), f32),
            shape(floe_drift_speed.shape, f32),
            shape(internal_tension_tensor.shape, f32),
        ),
        in_specs=[hbm] * 6 + [smem] * 2 + [hbm] * 4,
        out_specs=(hbm,) * 6,
        scratch_shapes=[
            like(warmth),
            pltpu.VMEM((places * BACK * 8, TILE), f32),
            pltpu.VMEM((places * EARLY * 8, TILE), f32),
            pltpu.VMEM((2, TILE, TILE), f32),
            pltpu.SMEM((3, n), jnp.int32),
            like(interface_conditions), like(floe_drift_speed), like(internal_tension_tensor),
            like(external_drive), like(floe_weight), like(floe_pressure),
            like(share), like(thick), like(drift),
            pltpu.VMEM((B, SENT * 8, TILE), f32),
            pltpu.VMEM((places * SENT * 8, TILE), f32),
            pltpu.VMEM((places * SENT * 8, TILE), f32),
            pltpu.VMEM((places * EARLY * 8, TILE), f32),
            pltpu.VMEM((places * BACK * 8, TILE), f32),
            pltpu.VMEM((EVP, ROWS, 2 * TILE), f32),
            pltpu.VMEM((TILE, TILE), f32),
            pltpu.VMEM((TILE, TILE), f32),
            pltpu.VMEM((EVP, HALO, TILE), f32),
            pltpu.VMEM((EVP, HALO, TILE), f32),
            pltpu.VMEM((TILE + 2 * HALO, TILE), f32),
            pltpu.VMEM((TILE + 2 * HALO, TILE), f32),
            pltpu.VMEM((EVP, HALO, TILE), f32),
            pltpu.VMEM((EVP, HALO, TILE), f32),
            dma((8,)), dma((BPX,)), dma((places // 8,)), dma((places // 8,)), dma((4,)), dma((n,)),
            dma((n,)), dma((n,)), dma((n,)), dma((n,)), dma((n,)), dma((n,)),
            dma((8,)), dma((8,)),
        ],
        compiler_params=pltpu.CompilerParams(
            collective_id=0, has_side_effects=True, vmem_limit_bytes=VMEM_LIMIT
        ),
    )(
        interface_conditions, floe_drift_speed, internal_tension_tensor, external_drive,
        floe_weight, floe_pressure, holder, ground_tile_marker, warmth, share, thick, drift,
    )
    warmth, exchanges, velocity, stress = pl.pallas_call(
        functools.partial(output_kernel, n),
        out_shape=tuple(
            shape(x.shape, f32) for x in (held, interface_conditions, velocity, stress)
        ),
        in_specs=[hbm] * 6 + [smem] * 2,
        out_specs=(hbm,) * 4,
        scratch_shapes=[
            like(held), like(got), like(got_early), like(coef), like(velocity), like(stress),
            like(interface_conditions), dma((2 * CLASSES + 5,)), dma((2 * CLASSES + 5 + BPX,)),
        ],
        compiler_params=pltpu.CompilerParams(vmem_limit_bytes=VMEM_LIMIT),
    )(held, got, got_early, coef, velocity, stress, holder, ground_tile_marker)
    return jnp.transpose(warmth, (2, 0, 1, 3)), exchanges, velocity, stress


def solution(mesh):
    tile = P(None, "gx", "gy")
    owner = ("gx", "gy")
    return jax.shard_map(
        local,
        mesh=mesh,
        in_specs=(
            tile, P(owner, None, None, None), P(owner, None, None), P(owner, None, None),
            P(owner, None, None), tile, tile, tile, P("gx", "gy"), P("gx", "gy"),
            P(owner, None), P(owner),
        ),
        out_specs=(P(owner, None, None, None), tile, tile, tile),
        check_vma=False,
    )
```
